32 devices in a mesh: dp: 4 (over y, x), expert: 8 (over z, core).
Axes of the slice: x: 2, y: 2, z: 4, core: 2. Of those that a mesh axis runs over, the one named last changes fastest.
Arguments:
- tokens: bfloat16 [4096, 2048], P(('dp', 'expert')), may hold values from -6 to 6
- cotangent: bfloat16 [4096, 2048], P(('dp', 'expert')), may hold values from -6 to 6
- expert_ids: int32 [4096, 2], P(('dp', 'expert')), may hold values from 0 to 7, all different within a row; in each aligned block of 128 rows (0 to 127, 128 to 255, ...) at most 40 rows name the same one
- gate_prob: float32 [4096, 2], P(('dp', 'expert')), may hold values from 0.2 to 1
- gate_weight: bfloat16 [8, 2048, 1408], P(None, 'expert', 'dp'), may hold values from -0.125 to 0.125
- up_weight: bfloat16 [8, 2048, 1408], P(None, 'expert', 'dp'), may hold values from -0.125 to 0.125
- down_weight: bfloat16 [8, 2048, 1408], P(None, 'expert', 'dp'), may hold values from -0.15625 to 0.15625
Outputs:
- mixed_out: bfloat16 [4096, 2048], P(('dp', 'expert'))
- grad_tokens: bfloat16 [4096, 2048], P(('dp', 'expert'))
- grad_gate: bfloat16 [8, 2048, 1408], P(None, 'expert', 'dp')
- grad_up: bfloat16 [8, 2048, 1408], P(None, 'expert', 'dp')
- grad_down: bfloat16 [8, 2048, 1408], P(None, 'expert', 'dp')
The draws below stay inside these ranges and needn't reach their ends.
Inputs may be any that keep to these rules, and one draw needn't show every extreme that they name: `expert_ids`: among the 128 rows of one device no expert is named by more than 40 pairs, and in some device's rows one expert is named by exactly 40.
All inputs are finite; a program needn't handle non-finite values.
Results may differ from the reference program's by a relative error of at most 0.011.
Values may be sent and summed in bfloat16 or wider, within the bound.
A program may use at most 192 MiB of HBM per device.

```python
import math
import jax
import jax.numpy as jnp
import numpy as np
from jax import lax

D = 2048
FF = 1408
TOPK = 2
TOK_DEV = 128
EXPERTS = 8
CAP = 40
TOKENS = 4096
N_DP = 4
N_EXPERT = 8


def level_of(own_key, dims, shards, least, largest):
    def one(axis_at, parts):
        draws = jax.random.uniform(jax.random.fold_in(jax.random.fold_in(own_key, 6), axis_at), (parts,), jnp.float32, least / len(shards), largest / len(shards))
        return jnp.repeat(jnp.exp(draws), dims[axis_at] // parts).reshape((-1,) + (1,) * (len(dims) - axis_at - 1))

    gain = one(*shards[0])
    for cut in shards[1:]:
        gain = gain * one(*cut)
    return gain


def routed_block(own_key, own, number, rows, amount, top, most, skew):
    ranking = jax.random.permutation(own_key, amount)
    heavy_load, ordinary = portions_of(amount, rows * top, most, skew, True), portions_of(amount, rows * top, most, skew, False)
    places = jnp.arange(amount)

    def named(tallies, offset_by):
        used = int((tallies > 0).sum())
        fixed = max(1, used // 4)
        shifted = fixed + (places - fixed + offset_by * (used - fixed)) % max(1, amount - fixed)
        return jnp.zeros((amount,), jnp.int32).at[ranking[jnp.where(places < fixed, places, shifted)]].set(jnp.asarray(tallies, jnp.int32))

    tallies = jnp.where(number % 4 == 0, named(heavy_load, number // 4), named(ordinary, number - number // 4 - 1))
    mixed = jax.random.permutation(jax.random.fold_in(own, 3), amount)
    donor, sink = mixed[0:amount // 2 * 2:2], mixed[1:amount // 2 * 2:2]
    room = jnp.minimum(tallies[donor] - 1, most - tallies[sink]) // 2
    room = jnp.where((donor == ranking[0]) | (sink == ranking[0]) | (tallies[sink] == 0), 0, jnp.maximum(room, 0))
    shifted = jax.random.randint(jax.random.fold_in(own, 4), (amount // 2,), 0, 1 << 20) % (room + 1)
    tallies = tallies.at[donor].add(-shifted).at[sink].add(shifted)
    labels = jnp.searchsorted(jnp.cumsum(tallies), jnp.arange(rows * top), side="right").astype(jnp.int32)
    listing = labels.reshape(top, rows).T
    listing = listing[jax.random.permutation(jax.random.fold_in(own, 1), rows)]
    offset_by = jax.random.randint(jax.random.fold_in(own, 2), (rows, 1), 0, top)
    return jnp.take_along_axis(listing, (jnp.arange(top)[None, :] + offset_by) % top, axis=1)


def portions_of(number_of, total, reach, slope, full):
    weights = [(1 << 20) // math.isqrt(standing ** slope) + 1 for standing in range(1, number_of + 1)]
    largest = reach if full else min(reach, max(-(-total // number_of), total * weights[0] // sum(weights)))
    least = 1 if total - largest >= number_of - 1 else 0
    counts, spare = [largest] + [least] * (number_of - 1), total - largest - least * (number_of - 1)
    while spare > 0:
        movable = [i for i in range(1, number_of) if counts[i] < largest] or [i for i in range(1, number_of) if counts[i] < reach]
        mass, left = sum([weights[i] for i in movable]), spare
        for i in movable:
            addition = min(reach - counts[i], max(1, left * weights[i] // mass), spare)
            counts[i] = counts[i] + addition
            spare = spare - addition
    return np.array(counts)


def noise(key, shape, deviation, limit, pieces=(), kind=jnp.bfloat16):
    drawn = deviation * jax.random.normal(key, shape, jnp.float32)
    if pieces:
        drawn = drawn * level_of(key, shape, pieces, -0.22, 0.18)
    return jnp.clip(drawn, -limit, limit).astype(kind)


def setup_inputs(seed: int = 0) -> dict:
    streams_of = jax.random.split(jax.random.key(seed), 8)
    tokens = noise(streams_of[0], (TOKENS, D), 1.0, 6.0, ((0, 32),))
    cotangent = noise(streams_of[1], (TOKENS, D), 1.0, 6.0, ((0, 32),))
    expert_ids_keys = jax.random.split(jax.random.fold_in(streams_of[2], 1), TOKENS // TOK_DEV)
    expert_ids_turns = jax.random.permutation(jax.random.fold_in(streams_of[2], 3), TOKENS // TOK_DEV)
    expert_ids = jax.vmap(lambda own, number: routed_block(jax.random.fold_in(streams_of[2], 2), own, number, TOK_DEV, EXPERTS, TOPK, CAP, 2))(expert_ids_keys, expert_ids_turns).reshape((TOKENS, TOPK))
    gate_prob = jnp.clip(0.2 + 0.8 * jax.random.uniform(streams_of[3], (TOKENS, TOPK), jnp.float32) ** level_of(streams_of[3], (TOKENS, TOPK), ((0, 32),), -0.2, 0.2), 0.2, 1.0)
    gate_weight = noise(streams_of[4], (EXPERTS, D, FF), D ** -0.5, 0.125, ((1, 8), (2, 4)))
    up_weight = noise(streams_of[5], (EXPERTS, D, FF), D ** -0.5, 0.125, ((1, 8), (2, 4)))
    down_weight = noise(streams_of[6], (EXPERTS, D, FF), FF ** -0.5, 0.15625, ((1, 8), (2, 4)))
    return dict(tokens=tokens, cotangent=cotangent, expert_ids=expert_ids, gate_prob=gate_prob, gate_weight=gate_weight, up_weight=up_weight, down_weight=down_weight)


def quarter_sum(products, portions):
    row_count = products[0][0].shape[0]
    col_count = products[0][1].shape[0]
    quarter_width = products[0][0].shape[1] // portions
    running = jnp.zeros((row_count, col_count), jnp.float32)
    for quarter in range(portions):
        lower = quarter * quarter_width
        upper = lower + quarter_width
        portion = jnp.zeros((row_count, col_count), jnp.float32)
        for left_mat, right_mat in products:
            portion = portion + lax.dot_general(left_mat[:, lower:upper], right_mat[:, lower:upper], (((1,), (1,)), ((), ())), preferred_element_type=jnp.float32)
        rounded = lax.optimization_barrier(portion.astype(jnp.bfloat16))
        running = running + rounded.astype(jnp.float32)
    return running


def reference(tokens, cotangent, expert_ids, gate_prob, gate_weight, up_weight, down_weight):
    pair_count = TOKENS * TOPK
    most_rows = N_DP * N_EXPERT * CAP
    flat_ids = expert_ids.reshape(-1)
    gate_scale = gate_prob.reshape(-1).astype(jnp.float32)
    pair_rows = jnp.repeat(tokens, TOPK, axis=0)
    pair_grads = (gate_scale[:, None] * jnp.repeat(cotangent, TOPK, axis=0).astype(jnp.float32)).astype(jnp.bfloat16)
    rows_pad = jnp.concatenate([pair_rows, jnp.zeros((1, D), jnp.bfloat16)], axis=0)
    grads_pad = jnp.concatenate([pair_grads, jnp.zeros((1, D), jnp.bfloat16)], axis=0)
    contracted = (((0,), (0,)), ((), ()))

    def one_expert(state_now, expert):
        out_rows, in_rows = state_now
        picked = jnp.nonzero(flat_ids == expert, size=most_rows, fill_value=pair_count)[0].astype(jnp.int32)
        rows_in = rows_pad[picked]
        cot_rows = grads_pad[picked]
        gate_mat = gate_weight[expert]
        up_mat = up_weight[expert]
        down_mat = down_weight[expert]
        pre_gate = jnp.dot(rows_in, gate_mat, preferred_element_type=jnp.float32)
        pre_up = jnp.dot(rows_in, up_mat, preferred_element_type=jnp.float32)
        hidden = (jax.nn.silu(pre_gate) * pre_up).astype(jnp.bfloat16)
        partial_value = quarter_sum(((hidden, down_mat),), N_DP).astype(jnp.bfloat16)
        hidden_grad = jnp.dot(cot_rows, down_mat, preferred_element_type=jnp.float32)
        squash = jax.nn.sigmoid(pre_gate)
        gate_grad = (hidden_grad * pre_up * (squash * (1.0 + pre_gate * (1.0 - squash)))).astype(jnp.bfloat16)
        up_grad = (hidden_grad * (pre_gate * squash)).astype(jnp.bfloat16)
        gate_total = lax.dot_general(rows_in, gate_grad, contracted, preferred_element_type=jnp.float32).astype(jnp.bfloat16)
        up_total = lax.dot_general(rows_in, up_grad, contracted, preferred_element_type=jnp.float32).astype(jnp.bfloat16)
        down_total = lax.dot_general(cot_rows, hidden, contracted, preferred_element_type=jnp.float32).astype(jnp.bfloat16)
        input_part = quarter_sum(((gate_grad, gate_mat), (up_grad, up_mat)), N_DP).astype(jnp.bfloat16)
        out_rows = out_rows.at[picked].set(partial_value)
        in_rows = in_rows.at[picked].set(input_part)
        return (out_rows, in_rows), (gate_total, up_total, down_total)

    start_state = (jnp.zeros((pair_count + 1, D), jnp.bfloat16), jnp.zeros((pair_count + 1, D), jnp.bfloat16))
    final_state, weight_grads = lax.scan(one_expert, start_state, jnp.arange(EXPERTS, dtype=jnp.int32))
    out_rows, in_rows = final_state
    expert_out = out_rows[:pair_count].astype(jnp.float32).reshape(TOKENS, TOPK, D)
    mixed_out = jnp.sum(gate_scale.reshape(TOKENS, TOPK, 1) * expert_out, axis=1).astype(jnp.bfloat16)
    grad_tokens = jnp.sum(in_rows[:pair_count].astype(jnp.float32).reshape(TOKENS, TOPK, D), axis=1).astype(jnp.bfloat16)
    return (mixed_out, grad_tokens, weight_grads[0], weight_grads[1], weight_grads[2])
```

```python
import functools

import jax
import jax.numpy as jnp
from jax import lax
from jax.experimental import pallas as pl
from jax.experimental.pallas import tpu as pltpu
from jax.sharding import PartitionSpec as P

TOPK = 2
VMEM_BYTES = 56 * 1024 * 1024


def slot_index(expert_ids, experts, capacity):
    flat_ids = expert_ids.reshape(-1)
    one_hot = (flat_ids[:, None] == jnp.arange(experts, dtype=jnp.int32)[None, :]).astype(jnp.int32)
    before = jnp.cumsum(one_hot, axis=0) - one_hot
    return flat_ids * capacity + jnp.sum(before * one_hot, axis=1)


def greet(ne, nd):
    me, row = lax.axis_index("expert"), lax.axis_index("dp")
    barrier = pltpu.get_barrier_semaphore()

    @pl.loop(1, ne)
    def _(s):
        pl.semaphore_signal(barrier, inc=1, device_id={"expert": lax.rem(me + s, ne)})

    @pl.loop(1, nd)
    def _(r):
        pl.semaphore_signal(barrier, inc=1, device_id={"dp": lax.rem(row + r, nd)})

    pl.semaphore_wait(barrier, ne - 1 + nd - 1)


def dispatch_kernel(
    ne, nd,
    rows, grads, gate, up, down,
    rows_out, grads_out, gate_out, up_out, down_out,
    pair_send, pair_recv, weight_send, weight_recv, fan_send, fan_recv, local_sem,
):
    me, row = lax.axis_index("expert"), lax.axis_index("dp")
    pairs = ((rows, rows_out), (grads, grads_out))
    weights = ((gate, gate_out), (up, up_out), (down, down_out))

    def peer(s):
        return lax.rem(me + s, ne)

    def source(s):
        return lax.rem(me - s + ne, ne)

    def pair_copy(k, s, landing):
        return pltpu.make_async_remote_copy(
            src_ref=pairs[k][0].at[peer(s)], dst_ref=pairs[k][1].at[row, landing],
            send_sem=pair_send.at[k, s], recv_sem=pair_recv.at[k, s],
            device_id={"expert": peer(s)},
        )

    def weight_copy(k, s, landing):
        return pltpu.make_async_remote_copy(
            src_ref=weights[k][0].at[peer(s)], dst_ref=weights[k][1].at[landing],
            send_sem=weight_send.at[k, s], recv_sem=weight_recv.at[k, s],
            device_id={"expert": peer(s)},
        )

    def fan_copy(k, s, r, src, landing):
        return pltpu.make_async_remote_copy(
            src_ref=src, dst_ref=pairs[k][1].at[landing, source(s)],
            send_sem=fan_send.at[k, r, s], recv_sem=fan_recv.at[k, r, s],
            device_id={"dp": lax.rem(row + r, nd)},
        )

    greet(ne, nd)

    @pl.loop(1, ne)
    def _(s):
        for k in range(2):
            pair_copy(k, s, me).start()

    local = [
        pltpu.make_async_copy(pairs[k][0].at[me], pairs[k][1].at[row, me], local_sem.at[k])
        for k in range(2)
    ] + [
        pltpu.make_async_copy(weights[k][0].at[me], weights[k][1].at[me], local_sem.at[2 + k])
        for k in range(3)
    ]
    for copy in local:
        copy.start()
    for k in range(2):
        for r in range(1, nd):
            fan_copy(k, 0, r, pairs[k][0].at[me], row).start()

    @pl.loop(1, ne)
    def _(s):
        for k in range(2):
            pair_copy(k, s, source(s)).wait_recv()
            for r in range(1, nd):
                fan_copy(k, s, r, pairs[k][1].at[row, source(s)], row).start()
        for k in range(3):
            weight_copy(k, s, me).start()

    for copy in local:
        copy.wait()

    @pl.loop(0, ne)
    def _(s):
        for k in range(2):
            for r in range(1, nd):
                arrived = fan_copy(
                    k, s, r, pairs[k][1].at[row, source(s)], lax.rem(row - r + nd, nd)
                )
                arrived.wait_send()
                arrived.wait_recv()

    @pl.loop(1, ne)
    def _(s):
        for k in range(2):
            pair_copy(k, s, me).wait_send()
        for k in range(3):
            weight_copy(k, s, source(s)).wait()


def combine_kernel(
    ne, nd,
    outs, ins, gate, up, down,
    outs_home, ins_home, gate_out, up_out, down_out,
    own, arrived, summed,
    home_send, home_recv, weight_send, weight_recv, fan_send, fan_recv, own_sem, local_sem,
):
    me, row = lax.axis_index("expert"), lax.axis_index("dp")
    parts = ((outs, outs_home), (ins, ins_home))
    weights = ((gate, gate_out), (up, up_out), (down, down_out))

    def peer(s):
        return lax.rem(me + s, ne)

    def source(s):
        return lax.rem(me - s + ne, ne)

    def home_copy(k, s, landing):
        return pltpu.make_async_remote_copy(
            src_ref=summed.at[k, peer(s)], dst_ref=parts[k][1].at[landing],
            send_sem=home_send.at[k, s], recv_sem=home_recv.at[k, s],
            device_id={"expert": peer(s)},
        )

    def weight_copy(k, s, landing):
        return pltpu.make_async_remote_copy(
            src_ref=weights[k][0].at[peer(s)], dst_ref=weights[k][1].at[landing],
            send_sem=weight_send.at[k, s], recv_sem=weight_recv.at[k, s],
            device_id={"expert": peer(s)},
        )

    def fan_copy(k, s, r):
        to = lax.rem(row + r, nd)
        return pltpu.make_async_remote_copy(
            src_ref=parts[k][0].at[to, peer(s)], dst_ref=arrived.at[k, r - 1, peer(s)],
            send_sem=fan_send.at[k, r, s], recv_sem=fan_recv.at[k, r, s],
            device_id={"dp": to},
        )

    def own_copy(k, s):
        return pltpu.make_async_copy(
            parts[k][0].at[row, peer(s)], own.at[k, peer(s)], own_sem.at[k, s]
        )

    greet(ne, nd)

    @pl.loop(1, ne)
    def _(s):
        for k in range(3):
            weight_copy(k, s, me).start()

    @pl.loop(1, ne + 1)
    def _(step):
        s = lax.rem(step, ne)
        for k in range(2):
            for r in range(1, nd):
                fan_copy(k, s, r).start()
            own_copy(k, s).start()

    local = [
        pltpu.make_async_copy(weights[k][0].at[me], weights[k][1].at[me], local_sem.at[k])
        for k in range(3)
    ]
    for copy in local:
        copy.start()

    def add_up(s):
        for k in range(2):
            own_copy(k, s).wait()
            total = own[k, peer(s)].astype(jnp.float32)
            for r in range(1, nd):
                fan_copy(k, s, r).wait_recv()
                total = total + arrived[k, r - 1, peer(s)].astype(jnp.float32)
            summed[k, peer(s)] = total.astype(jnp.bfloat16)

    @pl.loop(1, ne)
    def _(s):
        add_up(s)
        for k in range(2):
            home_copy(k, s, me).start()

    add_up(0)
    mine = [
        pltpu.make_async_copy(summed.at[k, me], parts[k][1].at[me], local_sem.at[3 + k])
        for k in range(2)
    ]
    for copy in mine:
        copy.start()
    for copy in local + mine:
        copy.wait()

    @pl.loop(0, ne)
    def _(s):
        for k in range(2):
            for r in range(1, nd):
                fan_copy(k, s, r).wait_send()

    @pl.loop(1, ne)
    def _(s):
        for k in range(2):
            home_copy(k, s, source(s)).wait()
        for k in range(3):
            weight_copy(k, s, source(s)).wait()


def comm_call(kernel, ne, nd, args, out_shape, scratch, collective_id):
    anywhere = pl.BlockSpec(memory_space=pl.ANY)
    return pl.pallas_call(
        functools.partial(kernel, ne, nd),
        out_shape=out_shape,
        in_specs=[anywhere] * len(args),
        out_specs=[anywhere] * len(out_shape),
        scratch_shapes=scratch,
        compiler_params=pltpu.CompilerParams(
            collective_id=collective_id, has_side_effects=True, vmem_limit_bytes=VMEM_BYTES
        ),
    )(*args)


def shards(ne, nd, tokens, cotangent, expert_ids, gate_prob, gate_weight, up_weight, down_weight):
    experts, depth, width = gate_weight.shape
    tok_rows, features = tokens.shape
    pair_count = tok_rows * TOPK
    capacity = max(2, 5 * pair_count // (4 * experts))
    slot_of = slot_index(expert_ids, experts, capacity)
    gate_scale = gate_prob.reshape(-1)
    slots = experts * capacity
    send_rows = (
        jnp.zeros((slots, features), jnp.bfloat16).at[slot_of].set(jnp.repeat(tokens, TOPK, axis=0))
    )
    scaled = (gate_scale[:, None] * jnp.repeat(cotangent, TOPK, axis=0).astype(jnp.float32)).astype(
        jnp.bfloat16
    )
    send_grads = jnp.zeros((slots, features), jnp.bfloat16).at[slot_of].set(scaled)
    slot_shape = (experts, capacity, features)
    dma = pltpu.SemaphoreType.DMA
    pair_type = jax.ShapeDtypeStruct((nd,) + slot_shape, jnp.bfloat16)
    home_type = jax.ShapeDtypeStruct(slot_shape, jnp.bfloat16)
    weight_type = jax.ShapeDtypeStruct(gate_weight.shape, jnp.bfloat16)
    rows, grads, gate, up, down = comm_call(
        dispatch_kernel, ne, nd,
        (send_rows.reshape(slot_shape), send_grads.reshape(slot_shape),
         gate_weight, up_weight, down_weight),
        [pair_type] * 2 + [weight_type] * 3,
        [dma((2, ne)), dma((2, ne)), dma((3, ne)), dma((3, ne)),
         dma((2, nd, ne)), dma((2, nd, ne)), dma((5,))],
        0,
    )
    total = nd * slots
    rows, grads = rows.reshape(total, features), grads.reshape(total, features)
    gate, up, down = (part.reshape(features, width) for part in (gate, up, down))
    contracted = (((0,), (0,)), ((), ()))
    turned = (((1,), (1,)), ((), ()))

    def dot(left, right, dims=(((1,), (0,)), ((), ()))):
        return lax.dot_general(left, right, dims, preferred_element_type=jnp.float32)

    pre_gate = dot(rows, gate)
    pre_up = dot(rows, up)
    hidden_grad = dot(grads, down)
    squash = jax.nn.sigmoid(pre_gate)
    hidden = (pre_gate * squash * pre_up).astype(jnp.bfloat16)
    gate_grad = (hidden_grad * pre_up * (squash * (1.0 + pre_gate * (1.0 - squash)))).astype(
        jnp.bfloat16
    )
    up_grad = (hidden_grad * (pre_gate * squash)).astype(jnp.bfloat16)
    totals = tuple(
        dot(left, right, contracted).astype(jnp.bfloat16).reshape(gate_weight.shape)
        for left, right in ((rows, gate_grad), (rows, up_grad), (grads, hidden))
    )
    outputs = dot(hidden, down, turned).astype(jnp.bfloat16)
    input_grads = (dot(gate_grad, gate, turned) + dot(up_grad, up, turned)).astype(jnp.bfloat16)
    out_home, in_home, grad_gate, grad_up, grad_down = comm_call(
        combine_kernel, ne, nd,
        (outputs.reshape((nd,) + slot_shape), input_grads.reshape((nd,) + slot_shape)) + totals,
        [home_type] * 2 + [weight_type] * 3,
        [pltpu.VMEM((2,) + slot_shape, jnp.bfloat16),
         pltpu.VMEM((2, nd - 1) + slot_shape, jnp.bfloat16),
         pltpu.VMEM((2,) + slot_shape, jnp.bfloat16),
         dma((2, ne)), dma((2, ne)), dma((3, ne)), dma((3, ne)),
         dma((2, nd, ne)), dma((2, nd, ne)), dma((2, ne)), dma((5,))],
        1,
    )
    out_pairs = out_home.reshape(slots, features)[slot_of].astype(jnp.float32)
    mixed_out = jnp.sum(
        (gate_scale[:, None] * out_pairs).reshape(tok_rows, TOPK, features), axis=1
    ).astype(jnp.bfloat16)
    in_pairs = in_home.reshape(slots, features)[slot_of].astype(jnp.float32)
    grad_tokens = jnp.sum(in_pairs.reshape(tok_rows, TOPK, features), axis=1).astype(jnp.bfloat16)
    return (mixed_out, grad_tokens, grad_gate, grad_up, grad_down)


def solution(mesh):
    by_token = P(("dp", "expert"), None)
    by_block = P(None, "expert", "dp")
    return jax.shard_map(
        functools.partial(shards, mesh.shape["expert"], mesh.shape["dp"]),
        mesh=mesh,
        in_specs=(by_token,) * 4 + (by_block,) * 3,
        out_specs=(by_token,) * 2 + (by_block,) * 3,
        check_vma=False,
    )
```

```python
import functools

import jax
import jax.numpy as jnp
from jax import lax
from jax.experimental import pallas as pl
from jax.experimental.pallas import tpu as pltpu
from jax.sharding import PartitionSpec as P

TOPK = 2
VMEM_BYTES = 60 * 1024 * 1024


def slot_index(expert_ids, experts, capacity):
    flat_ids = expert_ids.reshape(-1)
    one_hot = (flat_ids[:, None] == jnp.arange(experts, dtype=jnp.int32)[None, :]).astype(jnp.int32)
    before = jnp.cumsum(one_hot, axis=0) - one_hot
    return flat_ids * capacity + jnp.sum(before * one_hot, axis=1)


def greet(ne, nd):
    me, row = lax.axis_index("expert"), lax.axis_index("dp")
    barrier = pltpu.get_barrier_semaphore()

    @pl.loop(1, ne)
    def _(s):
        pl.semaphore_signal(barrier, inc=1, device_id={"expert": lax.rem(me + s, ne)})

    @pl.loop(1, nd)
    def _(r):
        pl.semaphore_signal(barrier, inc=1, device_id={"dp": lax.rem(row + r, nd)})

    pl.semaphore_wait(barrier, ne - 1 + nd - 1)


def weight_slot(ref, landing):
    if len(ref.shape) == 3:
        return ref.at[landing]
    return ref.at[:, columns_of(landing, ref.shape[1] // lax.axis_size("expert"))]


def columns_of(index, size):
    return pl.ds(pl.multiple_of(index * size, size), size)


def dispatch_kernel(
    ne, nd,
    rows, grads, gate, up, down,
    rows_out, grads_out, gate_out, up_out, down_out,
    pair_send, pair_recv, weight_send, weight_recv, fan_send, fan_recv, local_sem,
):
    me, row = lax.axis_index("expert"), lax.axis_index("dp")
    pairs = ((rows, rows_out), (grads, grads_out))
    weights = ((gate, gate_out), (up, up_out), (down, down_out))

    def peer(s):
        return lax.rem(me + s, ne)

    def source(s):
        return lax.rem(me - s + ne, ne)

    def pair_copy(k, s, landing):
        return pltpu.make_async_remote_copy(
            src_ref=pairs[k][0].at[peer(s)], dst_ref=pairs[k][1].at[row, landing],
            send_sem=pair_send.at[k, s], recv_sem=pair_recv.at[k, s],
            device_id={"expert": peer(s)},
        )

    def weight_copy(k, s, landing):
        return pltpu.make_async_remote_copy(
            src_ref=weights[k][0].at[peer(s)], dst_ref=weight_slot(weights[k][1], landing),
            send_sem=weight_send.at[k, s], recv_sem=weight_recv.at[k, s],
            device_id={"expert": peer(s)},
        )

    def fan_copy(k, s, r, src, landing):
        return pltpu.make_async_remote_copy(
            src_ref=src, dst_ref=pairs[k][1].at[landing, source(s)],
            send_sem=fan_send.at[k, r, s], recv_sem=fan_recv.at[k, r, s],
            device_id={"dp": lax.rem(row + r, nd)},
        )

    greet(ne, nd)

    @pl.loop(1, ne)
    def _(s):
        for k in range(2):
            pair_copy(k, s, me).start()

    local = [
        pltpu.make_async_copy(pairs[k][0].at[me], pairs[k][1].at[row, me], local_sem.at[k])
        for k in range(2)
    ] + [
        pltpu.make_async_copy(
            weights[k][0].at[me], weight_slot(weights[k][1], me), local_sem.at[2 + k]
        )
        for k in range(3)
    ]
    for copy in local:
        copy.start()
    for k in range(2):
        for r in range(1, nd):
            fan_copy(k, 0, r, pairs[k][0].at[me], row).start()

    @pl.loop(1, ne)
    def _(s):
        for k in range(2):
            pair_copy(k, s, source(s)).wait_recv()
            for r in range(1, nd):
                fan_copy(k, s, r, pairs[k][1].at[row, source(s)], row).start()
        for k in range(3):
            weight_copy(k, s, me).start()

    for copy in local:
        copy.wait()

    @pl.loop(0, ne)
    def _(s):
        for k in range(2):
            for r in range(1, nd):
                arrived = fan_copy(
                    k, s, r, pairs[k][1].at[row, source(s)], lax.rem(row - r + nd, nd)
                )
                arrived.wait_send()
                arrived.wait_recv()

    @pl.loop(1, ne)
    def _(s):
        for k in range(2):
            pair_copy(k, s, me).wait_send()
        for k in range(3):
            weight_copy(k, s, source(s)).wait()


def combine_kernel(
    ne, nd,
    outs, ins, gate, up, down,
    outs_home, ins_home, gate_out, up_out, down_out,
    own, arrived, summed,
    home_send, home_recv, weight_send, weight_recv, fan_send, fan_recv, own_sem, local_sem,
):
    me, row = lax.axis_index("expert"), lax.axis_index("dp")
    parts = ((outs, outs_home), (ins, ins_home))
    weights = ((gate, gate_out), (up, up_out), (down, down_out))

    def peer(s):
        return lax.rem(me + s, ne)

    def source(s):
        return lax.rem(me - s + ne, ne)

    def home_copy(k, s, landing):
        return pltpu.make_async_remote_copy(
            src_ref=summed.at[k, peer(s)], dst_ref=parts[k][1].at[landing],
            send_sem=home_send.at[k, s], recv_sem=home_recv.at[k, s],
            device_id={"expert": peer(s)},
        )

    def weight_copy(k, s, landing):
        return pltpu.make_async_remote_copy(
            src_ref=weights[k][0].at[peer(s)], dst_ref=weights[k][1].at[landing],
            send_sem=weight_send.at[k, s], recv_sem=weight_recv.at[k, s],
            device_id={"expert": peer(s)},
        )

    def fan_copy(k, s, r):
        to = lax.rem(row + r, nd)
        return pltpu.make_async_remote_copy(
            src_ref=parts[k][0].at[to, peer(s)], dst_ref=arrived.at[k, r - 1, peer(s)],
            send_sem=fan_send.at[k, r, s], recv_sem=fan_recv.at[k, r, s],
            device_id={"dp": to},
        )

    def own_copy(k, s):
        return pltpu.make_async_copy(
            parts[k][0].at[row, peer(s)], own.at[k, peer(s)], own_sem.at[k, s]
        )

    greet(ne, nd)

    @pl.loop(1, ne)
    def _(s):
        for k in range(3):
            weight_copy(k, s, me).start()

    @pl.loop(1, ne + 1)
    def _(step):
        s = lax.rem(step, ne)
        for k in range(2):
            for r in range(1, nd):
                fan_copy(k, s, r).start()
            own_copy(k, s).start()

    local = [
        pltpu.make_async_copy(weights[k][0].at[me], weights[k][1].at[me], local_sem.at[k])
        for k in range(3)
    ]
    for copy in local:
        copy.start()

    def add_up(s):
        for k in range(2):
            own_copy(k, s).wait()
            total = own[k, peer(s)].astype(jnp.float32)
            for r in range(1, nd):
                fan_copy(k, s, r).wait_recv()
                total = total + arrived[k, r - 1, peer(s)].astype(jnp.float32)
            summed[k, peer(s)] = total.astype(jnp.bfloat16)

    @pl.loop(1, ne)
    def _(s):
        add_up(s)
        for k in range(2):
            home_copy(k, s, me).start()

    add_up(0)
    mine = [
        pltpu.make_async_copy(summed.at[k, me], parts[k][1].at[me], local_sem.at[3 + k])
        for k in range(2)
    ]
    for copy in mine:
        copy.start()
    for copy in local + mine:
        copy.wait()

    @pl.loop(0, ne)
    def _(s):
        for k in range(2):
            for r in range(1, nd):
                fan_copy(k, s, r).wait_send()

    @pl.loop(1, ne)
    def _(s):
        for k in range(2):
            home_copy(k, s, source(s)).wait()
        for k in range(3):
            weight_copy(k, s, source(s)).wait()


def fused_combine_kernel(
    ne, nd,
    rows, grads, gate, up, down, gate_grad, up_grad, hidden, gate_turned, up_turned, hidden_turned,
    slots, scale,
    mixed_out, token_out, gate_out, up_out, down_out,
    rows_in, grads_in, gate_in, up_in, down_in, gate_grad_in, up_grad_in, hidden_in,
    gate_turned_in, up_turned_in, hidden_turned_in,
    made, part, arrived, summed, home,
    home_send, home_recv, weight_send, weight_recv, fan_send, fan_recv, load_sem, local_sem,
):
    me, row = lax.axis_index("expert"), lax.axis_index("dp")
    weight_outs = (gate_out, up_out, down_out)
    features = rows.shape[1]
    depth = features // ne
    cap = part.shape[3]
    block = ne * cap

    def peer(s):
        return lax.rem(me + s, ne)

    def source(s):
        return lax.rem(me - s + ne, ne)

    def home_copy(k, s, landing):
        return pltpu.make_async_remote_copy(
            src_ref=summed.at[k, peer(s)], dst_ref=home.at[k, landing],
            send_sem=home_send.at[k, s], recv_sem=home_recv.at[k, s],
            device_id={"expert": peer(s)},
        )

    def weight_copy(k, s, landing):
        return pltpu.make_async_remote_copy(
            src_ref=made.at[k, peer(s)], dst_ref=weight_outs[k].at[landing],
            send_sem=weight_send.at[k, s], recv_sem=weight_recv.at[k, s],
            device_id={"expert": peer(s)},
        )

    def fan_copy(k, s, r):
        to = lax.rem(row + r, nd)
        return pltpu.make_async_remote_copy(
            src_ref=part.at[k, to, peer(s)], dst_ref=arrived.at[k, r - 1, peer(s)],
            send_sem=fan_send.at[k, r, s], recv_sem=fan_recv.at[k, r, s],
            device_id={"dp": to},
        )

    loads = [
        pltpu.make_async_copy(src, dst, load_sem.at[at])
        for at, (src, dst) in enumerate((
            (gate_turned, gate_turned_in), (rows, rows_in), (up_turned, up_turned_in),
            (hidden_turned, hidden_turned_in), (grads, grads_in),
            (hidden, hidden_in), (down, down_in), (gate_grad, gate_grad_in), (gate, gate_in),
            (up_grad, up_grad_in), (up, up_in),
        ))
    ]
    for load in loads:
        load.start()
    greet(ne, nd)
    for load in loads:
        load.wait()

    def dot(left, right):
        return jnp.dot(left, right, preferred_element_type=jnp.float32)

    def make_weights(s):
        columns = columns_of(peer(s), depth)
        rows_now, grads_now = rows_in[:, columns], grads_in[:, columns]
        made[0, peer(s)] = dot(gate_turned_in[...], rows_now).astype(jnp.bfloat16)
        made[1, peer(s)] = dot(up_turned_in[...], rows_now).astype(jnp.bfloat16)
        made[2, peer(s)] = dot(hidden_turned_in[...], grads_now).astype(jnp.bfloat16)

    def make_parts(to):
        lines = columns_of(to, block)

        @pl.loop(0, features // 256)
        def _(tile):
            columns = columns_of(tile, 256)
            outs = dot(hidden_in[lines, :], down_in[:, columns])
            ins = dot(gate_grad_in[lines, :], gate_in[:, columns]) + dot(
                up_grad_in[lines, :], up_in[:, columns]
            )
            for e in range(ne):
                part[0, to, e, :, columns] = outs[e * cap : (e + 1) * cap].astype(jnp.bfloat16)
                part[1, to, e, :, columns] = ins[e * cap : (e + 1) * cap].astype(jnp.bfloat16)

    @pl.loop(1, ne)
    def _(s):
        make_weights(s)
        for k in range(3):
            weight_copy(k, s, me).start()

        @pl.when(s < nd)
        def _():
            make_parts(lax.rem(row + s, nd))

            @pl.loop(1, ne + 1)
            def _(step):
                for k in range(2):
                    fan_copy(k, lax.rem(step, ne), s).start()

    make_parts(row)
    make_weights(0)
    local = [
        pltpu.make_async_copy(made.at[k, me], weight_outs[k].at[me], local_sem.at[k])
        for k in range(3)
    ]
    for copy in local:
        copy.start()

    def add_up(s, target):
        for k in range(2):
            for r in range(1, nd):
                fan_copy(k, s, r).wait_recv()

            @pl.loop(0, features // 256)
            def _(tile):
                columns = columns_of(tile, 256)
                total = part[k, row, peer(s), :, columns].astype(jnp.float32)
                for r in range(1, nd):
                    total = total + arrived[k, r - 1, peer(s), :, columns].astype(jnp.float32)
                target[k, peer(s), :, columns] = total.astype(jnp.bfloat16)

    @pl.loop(1, ne)
    def _(s):
        add_up(s, summed)
        for k in range(2):
            home_copy(k, s, me).start()

    add_up(0, home)
    for copy in local:
        copy.wait()

    @pl.loop(0, ne)
    def _(s):
        for k in range(2):
            for r in range(1, nd):
                fan_copy(k, s, r).wait_send()

    @pl.loop(1, ne)
    def _(s):
        for k in range(2):
            home_copy(k, s, source(s)).wait()

    tok_rows = slots.shape[0]
    places = lax.broadcasted_iota(jnp.int32, (tok_rows, block), 1)
    chosen = [
        jnp.where(places == slots[:, k : k + 1], 1.0, 0.0).astype(jnp.float32) for k in range(TOPK)
    ]
    either = (chosen[0] + chosen[1]).astype(jnp.bfloat16)
    first, second = (one.astype(jnp.bfloat16) for one in chosen)
    first_scale, second_scale = scale[:, 0:1], scale[:, 1:2]

    def at_home(k, columns):
        return jnp.concatenate(
            [home[k, e, :, columns].astype(jnp.float32) for e in range(ne)], axis=0
        ).astype(jnp.bfloat16)

    @pl.loop(0, features // 256)
    def _(tile):
        columns = columns_of(tile, 256)
        outs = at_home(0, columns)
        mixed_out[:, columns] = (
            first_scale * dot(first, outs) + second_scale * dot(second, outs)
        ).astype(jnp.bfloat16)
        token_out[:, columns] = dot(either, at_home(1, columns)).astype(jnp.bfloat16)

    @pl.loop(1, ne)
    def _(s):
        for k in range(3):
            weight_copy(k, s, source(s)).wait()


def fused_combine(ne, nd, capacity, args, weight_type):
    rows, gate, turned, slots = args[0], args[2], args[8], args[11]
    features = rows.shape[1]
    anywhere, inside = pl.BlockSpec(memory_space=pl.ANY), pl.BlockSpec(memory_space=pltpu.VMEM)
    token_type = jax.ShapeDtypeStruct((slots.shape[0], features), jnp.bfloat16)
    dma = pltpu.SemaphoreType.DMA
    block = (ne, capacity, features)
    return pl.pallas_call(
        functools.partial(fused_combine_kernel, ne, nd),
        out_shape=[token_type] * 2 + [weight_type] * 3,
        in_specs=[anywhere] * 11 + [inside] * 2,
        out_specs=[inside] * 2 + [anywhere] * 3,
        scratch_shapes=[pltpu.VMEM(part.shape, part.dtype) for part in args[:11]] + [
            pltpu.VMEM((3,) + weight_type.shape, jnp.bfloat16),
            pltpu.VMEM((2, nd) + block, jnp.bfloat16),
            pltpu.VMEM((2, nd - 1) + block, jnp.bfloat16),
            pltpu.VMEM((2,) + block, jnp.bfloat16),
            pltpu.VMEM((2,) + block, jnp.bfloat16),
            dma((2, ne)), dma((2, ne)), dma((3, ne)), dma((3, ne)),
            dma((2, nd, ne)), dma((2, nd, ne)), dma((11,)), dma((3,)),
        ],
        compiler_params=pltpu.CompilerParams(
            collective_id=1, has_side_effects=True, vmem_limit_bytes=VMEM_BYTES
        ),
    )(*args)


def comm_call(kernel, ne, nd, args, out_shape, scratch, collective_id):
    anywhere = pl.BlockSpec(memory_space=pl.ANY)
    return pl.pallas_call(
        functools.partial(kernel, ne, nd),
        out_shape=out_shape,
        in_specs=[anywhere] * len(args),
        out_specs=[anywhere] * len(out_shape),
        scratch_shapes=scratch,
        compiler_params=pltpu.CompilerParams(
            collective_id=collective_id, has_side_effects=True, vmem_limit_bytes=VMEM_BYTES
        ),
    )(*args)


def shards(ne, nd, tokens, cotangent, expert_ids, gate_prob, gate_weight, up_weight, down_weight):
    experts, depth, width = gate_weight.shape
    tok_rows, features = tokens.shape
    pair_count = tok_rows * TOPK
    capacity = max(2, 5 * pair_count // (4 * experts))
    slot_of = slot_index(expert_ids, experts, capacity)
    gate_scale = gate_prob.reshape(-1)
    slots = experts * capacity
    send_rows = (
        jnp.zeros((slots, features), jnp.bfloat16).at[slot_of].set(jnp.repeat(tokens, TOPK, axis=0))
    )
    scaled = (gate_scale[:, None] * jnp.repeat(cotangent, TOPK, axis=0).astype(jnp.float32)).astype(
        jnp.bfloat16
    )
    send_grads = jnp.zeros((slots, features), jnp.bfloat16).at[slot_of].set(scaled)
    slot_shape = (experts, capacity, features)
    dma = pltpu.SemaphoreType.DMA
    pair_type = jax.ShapeDtypeStruct((nd,) + slot_shape, jnp.bfloat16)
    home_type = jax.ShapeDtypeStruct(slot_shape, jnp.bfloat16)
    aligned = depth % 256 == 0 and capacity % 8 == 0 and width % 16 == 0
    weights = (gate_weight, up_weight, down_weight)
    if aligned:
        weights = tuple(part.transpose(0, 2, 1) for part in weights)
        landed_type = jax.ShapeDtypeStruct((width, features), jnp.bfloat16)
    else:
        landed_type = jax.ShapeDtypeStruct(gate_weight.shape, jnp.bfloat16)
    weight_type = jax.ShapeDtypeStruct(weights[0].shape, jnp.bfloat16)
    rows, grads, gate, up, down = comm_call(
        dispatch_kernel, ne, nd,
        (send_rows.reshape(slot_shape), send_grads.reshape(slot_shape)) + weights,
        [pair_type] * 2 + [landed_type] * 3,
        [dma((2, ne)), dma((2, ne)), dma((3, ne)), dma((3, ne)),
         dma((2, nd, ne)), dma((2, nd, ne)), dma((5,))],
        0,
    )
    total = nd * slots
    rows, grads = rows.reshape(total, features), grads.reshape(total, features)
    if not aligned:
        gate, up, down = (part.reshape(features, width) for part in (gate, up, down))
    contracted = (((0,), (0,)), ((), ()))
    turned = (((1,), (1,)), ((), ()))

    def dot(left, right, dims):
        return lax.dot_general(left, right, dims, preferred_element_type=jnp.float32)

    ahead = turned if aligned else (((1,), (0,)), ((), ()))
    pre_gate = dot(rows, gate, ahead)
    pre_up = dot(rows, up, ahead)
    hidden_grad = dot(grads, down, ahead)
    squash = jax.nn.sigmoid(pre_gate)
    hidden = (pre_gate * squash * pre_up).astype(jnp.bfloat16)
    gate_grad = (hidden_grad * pre_up * (squash * (1.0 + pre_gate * (1.0 - squash)))).astype(
        jnp.bfloat16
    )
    up_grad = (hidden_grad * (pre_gate * squash)).astype(jnp.bfloat16)
    if aligned:
        mixed_out, grad_tokens, *weight_grads = fused_combine(
            ne, nd, capacity,
            (rows, grads, gate, up, down, gate_grad, up_grad, hidden,
             gate_grad.T, up_grad.T, hidden.T, slot_of.reshape(tok_rows, TOPK), gate_prob),
            weight_type,
        )
        return (mixed_out, grad_tokens, *(part.transpose(0, 2, 1) for part in weight_grads))
    totals = tuple(
        dot(left, right, contracted).astype(jnp.bfloat16).reshape(gate_weight.shape)
        for left, right in ((rows, gate_grad), (rows, up_grad), (grads, hidden))
    )
    outputs = dot(hidden, down, turned).astype(jnp.bfloat16)
    input_grads = (dot(gate_grad, gate, turned) + dot(up_grad, up, turned)).astype(jnp.bfloat16)
    out_home, in_home, grad_gate, grad_up, grad_down = comm_call(
        combine_kernel, ne, nd,
        (outputs.reshape((nd,) + slot_shape), input_grads.reshape((nd,) + slot_shape)) + totals,
        [home_type] * 2 + [weight_type] * 3,
        [pltpu.VMEM((2,) + slot_shape, jnp.bfloat16),
         pltpu.VMEM((2, nd - 1) + slot_shape, jnp.bfloat16),
         pltpu.VMEM((2,) + slot_shape, jnp.bfloat16),
         dma((2, ne)), dma((2, ne)), dma((3, ne)), dma((3, ne)),
         dma((2, nd, ne)), dma((2, nd, ne)), dma((2, ne)), dma((5,))],
        1,
    )
    out_pairs = out_home.reshape(slots, features)[slot_of].astype(jnp.float32)
    mixed_out = jnp.sum(
        (gate_scale[:, None] * out_pairs).reshape(tok_rows, TOPK, features), axis=1
    ).astype(jnp.bfloat16)
    in_pairs = in_home.reshape(slots, features)[slot_of].astype(jnp.float32)
    grad_tokens = jnp.sum(in_pairs.reshape(tok_rows, TOPK, features), axis=1).astype(jnp.bfloat16)
    return (mixed_out, grad_tokens, grad_gate, grad_up, grad_down)


def solution(mesh):
    by_token = P(("dp", "expert"), None)
    by_block = P(None, "expert", "dp")
    return jax.shard_map(
        functools.partial(shards, mesh.shape["expert"], mesh.shape["dp"]),
        mesh=mesh,
        in_specs=(by_token,) * 4 + (by_block,) * 3,
        out_specs=(by_token,) * 2 + (by_block,) * 3,
        check_vma=False,
    )
```

```python
import functools

import jax
import jax.numpy as jnp
from jax import lax
from jax.experimental import pallas as pl
from jax.experimental.pallas import tpu as pltpu
from jax.sharding import PartitionSpec as P

TOPK = 2
VMEM_BYTES = 60 * 1024 * 1024


def slot_index(expert_ids, experts, capacity):
    flat_ids = expert_ids.reshape(-1)
    one_hot = (flat_ids[:, None] == jnp.arange(experts, dtype=jnp.int32)[None, :]).astype(jnp.int32)
    before = jnp.cumsum(one_hot, axis=0) - one_hot
    return flat_ids * capacity + jnp.sum(before * one_hot, axis=1)


def greet(ne, nd):
    me, row = lax.axis_index("expert"), lax.axis_index("dp")
    barrier = pltpu.get_barrier_semaphore()

    @pl.loop(1, ne)
    def _(s):
        pl.semaphore_signal(barrier, inc=1, device_id={"expert": lax.rem(me + s, ne)})

    @pl.loop(1, nd)
    def _(r):
        pl.semaphore_signal(barrier, inc=1, device_id={"dp": lax.rem(row + r, nd)})

    pl.semaphore_wait(barrier, ne - 1 + nd - 1)


def weight_slot(ref, landing):
    if len(ref.shape) == 3:
        return ref.at[landing]
    return ref.at[:, columns_of(landing, ref.shape[1] // lax.axis_size("expert"))]


def dot(left, right):
    return jnp.dot(left, right, preferred_element_type=jnp.float32)


def dot_turned(left, right):
    return lax.dot_general(
        left, right, (((1,), (1,)), ((), ())), preferred_element_type=jnp.float32
    )


def columns_of(index, size):
    return pl.ds(pl.multiple_of(index * size, size), size)


def dispatch_kernel(
    ne, nd,
    rows, grads, gate, up, down,
    rows_out, grads_out, gate_out, up_out, down_out,
    pair_send, pair_recv, weight_send, weight_recv, fan_send, fan_recv, local_sem,
):
    me, row = lax.axis_index("expert"), lax.axis_index("dp")
    pairs = ((rows, rows_out), (grads, grads_out))
    weights = ((gate, gate_out), (up, up_out), (down, down_out))

    def peer(s):
        return lax.rem(me + s, ne)

    def source(s):
        return lax.rem(me - s + ne, ne)

    def pair_copy(k, s, landing):
        return pltpu.make_async_remote_copy(
            src_ref=pairs[k][0].at[peer(s)], dst_ref=pairs[k][1].at[row, landing],
            send_sem=pair_send.at[k, s], recv_sem=pair_recv.at[k, s],
            device_id={"expert": peer(s)},
        )

    def weight_copy(k, s, landing):
        return pltpu.make_async_remote_copy(
            src_ref=weights[k][0].at[peer(s)], dst_ref=weight_slot(weights[k][1], landing),
            send_sem=weight_send.at[k, s], recv_sem=weight_recv.at[k, s],
            device_id={"expert": peer(s)},
        )

    def fan_copy(k, s, r, src, landing):
        return pltpu.make_async_remote_copy(
            src_ref=src, dst_ref=pairs[k][1].at[landing, source(s)],
            send_sem=fan_send.at[k, r, s], recv_sem=fan_recv.at[k, r, s],
            device_id={"dp": lax.rem(row + r, nd)},
        )

    greet(ne, nd)

    @pl.loop(1, ne)
    def _(s):
        for k in range(2):
            pair_copy(k, s, me).start()

    local = [
        pltpu.make_async_copy(pairs[k][0].at[me], pairs[k][1].at[row, me], local_sem.at[k])
        for k in range(2)
    ] + [
        pltpu.make_async_copy(
            weights[k][0].at[me], weight_slot(weights[k][1], me), local_sem.at[2 + k]
        )
        for k in range(3)
    ]
    for copy in local:
        copy.start()
    for k in range(2):
        for r in range(1, nd):
            fan_copy(k, 0, r, pairs[k][0].at[me], row).start()

    @pl.loop(1, ne)
    def _(s):
        for k in range(2):
            pair_copy(k, s, source(s)).wait_recv()
            for r in range(1, nd):
                fan_copy(k, s, r, pairs[k][1].at[row, source(s)], row).start()
        for k in range(3):
            weight_copy(k, s, me).start()

    for copy in local:
        copy.wait()

    @pl.loop(0, ne)
    def _(s):
        for k in range(2):
            for r in range(1, nd):
                arrived = fan_copy(
                    k, s, r, pairs[k][1].at[row, source(s)], lax.rem(row - r + nd, nd)
                )
                arrived.wait_send()
                arrived.wait_recv()

    @pl.loop(1, ne)
    def _(s):
        for k in range(2):
            pair_copy(k, s, me).wait_send()
        for k in range(3):
            weight_copy(k, s, source(s)).wait()


def fused_dispatch_kernel(
    ne, nd,
    tokens, cotangent, ids_turned, scale, gate, up, down,
    rows_out, grads_out, gate_out, up_out, down_out,
    rows, grads,
    pair_send, pair_recv, weight_send, weight_recv, fan_send, fan_recv, local_sem,
):
    me, row = lax.axis_index("expert"), lax.axis_index("dp")
    pairs = ((rows, rows_out), (grads, grads_out))
    weights = ((gate, gate_out), (up, up_out), (down, down_out))

    early = min(3, ne)

    def peer(s):
        return lax.rem(me + s, ne)

    def source(s):
        return lax.rem(me - s + ne, ne)

    def pair_copy(k, s, landing):
        return pltpu.make_async_remote_copy(
            src_ref=pairs[k][0].at[peer(s)], dst_ref=pairs[k][1].at[row, landing],
            send_sem=pair_send.at[k, s], recv_sem=pair_recv.at[k, s],
            device_id={"expert": peer(s)},
        )

    def weight_copy(k, s, landing):
        return pltpu.make_async_remote_copy(
            src_ref=weights[k][0].at[peer(s)], dst_ref=weight_slot(weights[k][1], landing),
            send_sem=weight_send.at[k, s], recv_sem=weight_recv.at[k, s],
            device_id={"expert": peer(s)},
        )

    def fan_copy(k, s, r, src, landing):
        return pltpu.make_async_remote_copy(
            src_ref=src, dst_ref=pairs[k][1].at[landing, source(s)],
            send_sem=fan_send.at[k, r, s], recv_sem=fan_recv.at[k, r, s],
            device_id={"dp": lax.rem(row + r, nd)},
        )

    greet(ne, nd)

    @pl.loop(1, early)
    def _(s):
        for k in range(3):
            weight_copy(k, s, me).start()

    cap, features = rows.shape[1:]
    tok_rows = tokens.shape[0]
    experts = lax.broadcasted_iota(jnp.int32, (ne, tok_rows), 0)
    named = [jnp.where(experts == ids_turned[k : k + 1, :], 1.0, 0.0) for k in range(TOPK)]
    earlier = jnp.where(
        lax.broadcasted_iota(jnp.int32, (tok_rows, tok_rows), 0)
        < lax.broadcasted_iota(jnp.int32, (tok_rows, tok_rows), 1), 1.0, 0.0
    ).astype(jnp.bfloat16)
    rank = dot((named[0] + named[1]).astype(jnp.bfloat16), earlier)
    place = rank + (experts * cap).astype(jnp.float32)
    slots = lax.broadcasted_iota(jnp.int32, (ne * cap, tok_rows), 0).astype(jnp.float32)
    first, second = (
        jnp.where(slots == jnp.sum(one * place, axis=0, keepdims=True), 1.0, 0.0) for one in named
    )
    either = (first + second).astype(jnp.bfloat16)
    first, second = first.astype(jnp.bfloat16), second.astype(jnp.bfloat16)

    @pl.loop(0, features // 256)
    def _(tile):
        columns = columns_of(tile, 256)
        cot = cotangent[:, columns].astype(jnp.float32)
        picked = dot(either, tokens[:, columns])
        picked_grads = dot(first, (scale[:, 0:1] * cot).astype(jnp.bfloat16)) + dot(
            second, (scale[:, 1:2] * cot).astype(jnp.bfloat16)
        )
        for e in range(ne):
            rows[e, :, columns] = picked[e * cap : (e + 1) * cap].astype(jnp.bfloat16)
            grads[e, :, columns] = picked_grads[e * cap : (e + 1) * cap].astype(jnp.bfloat16)

    @pl.loop(1, ne)
    def _(s):
        for k in range(2):
            pair_copy(k, s, me).start()

    local = [
        pltpu.make_async_copy(pairs[k][0].at[me], pairs[k][1].at[row, me], local_sem.at[k])
        for k in range(2)
    ] + [
        pltpu.make_async_copy(
            weights[k][0].at[me], weight_slot(weights[k][1], me), local_sem.at[2 + k]
        )
        for k in range(3)
    ]
    for copy in local:
        copy.start()
    for k in range(2):
        for r in range(1, nd):
            fan_copy(k, 0, r, pairs[k][0].at[me], row).start()

    @pl.loop(1, ne)
    def _(s):
        for k in range(2):
            pair_copy(k, s, source(s)).wait_recv()
            for r in range(1, nd):
                fan_copy(k, s, r, pairs[k][1].at[row, source(s)], row).start()
        @pl.when(s >= early)
        def _():
            for k in range(3):
                weight_copy(k, s, me).start()

    for copy in local:
        copy.wait()

    @pl.loop(0, ne)
    def _(s):
        for k in range(2):
            for r in range(1, nd):
                arrived = fan_copy(
                    k, s, r, pairs[k][1].at[row, source(s)], lax.rem(row - r + nd, nd)
                )
                arrived.wait_send()
                arrived.wait_recv()

    @pl.loop(1, ne)
    def _(s):
        for k in range(2):
            pair_copy(k, s, me).wait_send()
        for k in range(3):
            weight_copy(k, s, source(s)).wait()


def fused_dispatch(ne, nd, capacity, args, pair_type, landed_type):
    anywhere, inside = pl.BlockSpec(memory_space=pl.ANY), pl.BlockSpec(memory_space=pltpu.VMEM)
    dma = pltpu.SemaphoreType.DMA
    block = pair_type.shape[1:]
    return pl.pallas_call(
        functools.partial(fused_dispatch_kernel, ne, nd),
        out_shape=[pair_type] * 2 + [landed_type] * 3,
        in_specs=[inside] * 4 + [anywhere] * 3,
        out_specs=[anywhere] * 5,
        scratch_shapes=[
            pltpu.VMEM(block, jnp.bfloat16), pltpu.VMEM(block, jnp.bfloat16),
            dma((2, ne)), dma((2, ne)), dma((3, ne)), dma((3, ne)),
            dma((2, nd, ne)), dma((2, nd, ne)), dma((5,)),
        ],
        compiler_params=pltpu.CompilerParams(
            collective_id=2, has_side_effects=True, vmem_limit_bytes=VMEM_BYTES
        ),
    )(*args)


def combine_kernel(
    ne, nd,
    outs, ins, gate, up, down,
    outs_home, ins_home, gate_out, up_out, down_out,
    own, arrived, summed,
    home_send, home_recv, weight_send, weight_recv, fan_send, fan_recv, own_sem, local_sem,
):
    me, row = lax.axis_index("expert"), lax.axis_index("dp")
    parts = ((outs, outs_home), (ins, ins_home))
    weights = ((gate, gate_out), (up, up_out), (down, down_out))

    def peer(s):
        return lax.rem(me + s, ne)

    def source(s):
        return lax.rem(me - s + ne, ne)

    def home_copy(k, s, landing):
        return pltpu.make_async_remote_copy(
            src_ref=summed.at[k, peer(s)], dst_ref=parts[k][1].at[landing],
            send_sem=home_send.at[k, s], recv_sem=home_recv.at[k, s],
            device_id={"expert": peer(s)},
        )

    def weight_copy(k, s, landing):
        return pltpu.make_async_remote_copy(
            src_ref=weights[k][0].at[peer(s)], dst_ref=weights[k][1].at[landing],
            send_sem=weight_send.at[k, s], recv_sem=weight_recv.at[k, s],
            device_id={"expert": peer(s)},
        )

    def fan_copy(k, s, r):
        to = lax.rem(row + r, nd)
        return pltpu.make_async_remote_copy(
            src_ref=parts[k][0].at[to, peer(s)], dst_ref=arrived.at[k, r - 1, peer(s)],
            send_sem=fan_send.at[k, r, s], recv_sem=fan_recv.at[k, r, s],
            device_id={"dp": to},
        )

    def own_copy(k, s):
        return pltpu.make_async_copy(
            parts[k][0].at[row, peer(s)], own.at[k, peer(s)], own_sem.at[k, s]
        )

    greet(ne, nd)

    @pl.loop(1, ne)
    def _(s):
        for k in range(3):
            weight_copy(k, s, me).start()

    @pl.loop(1, ne + 1)
    def _(step):
        s = lax.rem(step, ne)
        for k in range(2):
            for r in range(1, nd):
                fan_copy(k, s, r).start()
            own_copy(k, s).start()

    local = [
        pltpu.make_async_copy(weights[k][0].at[me], weights[k][1].at[me], local_sem.at[k])
        for k in range(3)
    ]
    for copy in local:
        copy.start()

    def add_up(s):
        for k in range(2):
            own_copy(k, s).wait()
            total = own[k, peer(s)].astype(jnp.float32)
            for r in range(1, nd):
                fan_copy(k, s, r).wait_recv()
                total = total + arrived[k, r - 1, peer(s)].astype(jnp.float32)
            summed[k, peer(s)] = total.astype(jnp.bfloat16)

    @pl.loop(1, ne)
    def _(s):
        add_up(s)
        for k in range(2):
            home_copy(k, s, me).start()

    add_up(0)
    mine = [
        pltpu.make_async_copy(summed.at[k, me], parts[k][1].at[me], local_sem.at[3 + k])
        for k in range(2)
    ]
    for copy in mine:
        copy.start()
    for copy in local + mine:
        copy.wait()

    @pl.loop(0, ne)
    def _(s):
        for k in range(2):
            for r in range(1, nd):
                fan_copy(k, s, r).wait_send()

    @pl.loop(1, ne)
    def _(s):
        for k in range(2):
            home_copy(k, s, source(s)).wait()
        for k in range(3):
            weight_copy(k, s, source(s)).wait()


def fused_combine_kernel(
    ne, nd,
    rows, grads, gate, up, down, ids, scale,
    mixed_out, token_out, gate_out, up_out, down_out,
    rows_in, grads_in, gate_in, up_in, down_in, gate_grad_in, up_grad_in, hidden_in,
    gate_turned_in, up_turned_in, hidden_turned_in,
    made, part, arrived, summed, home,
    home_send, home_recv, weight_send, weight_recv, fan_send, fan_recv, load_sem, local_sem,
):
    me, row = lax.axis_index("expert"), lax.axis_index("dp")
    weight_outs = (gate_out, up_out, down_out)
    features = rows.shape[1]
    depth = features // ne
    cap = part.shape[3]
    block = ne * cap

    def peer(s):
        return lax.rem(me + s, ne)

    def source(s):
        return lax.rem(me - s + ne, ne)

    def home_copy(k, s, landing):
        return pltpu.make_async_remote_copy(
            src_ref=summed.at[k, peer(s)], dst_ref=home.at[k, landing],
            send_sem=home_send.at[k, s], recv_sem=home_recv.at[k, s],
            device_id={"expert": peer(s)},
        )

    def weight_copy(k, s, landing):
        return pltpu.make_async_remote_copy(
            src_ref=made.at[k, peer(s)], dst_ref=weight_outs[k].at[landing],
            send_sem=weight_send.at[k, s], recv_sem=weight_recv.at[k, s],
            device_id={"expert": peer(s)},
        )

    def fan_copy(k, s, r):
        to = lax.rem(row + r, nd)
        return pltpu.make_async_remote_copy(
            src_ref=part.at[k, to, peer(s)], dst_ref=arrived.at[k, r - 1, peer(s)],
            send_sem=fan_send.at[k, r, s], recv_sem=fan_recv.at[k, r, s],
            device_id={"dp": to},
        )

    loads = [
        pltpu.make_async_copy(src, dst, load_sem.at[at])
        for at, (src, dst) in enumerate((
            (gate, gate_in), (up, up_in), (down, down_in), (rows, rows_in), (grads, grads_in),
        ))
    ]
    for load in loads:
        load.start()
    greet(ne, nd)
    for load in loads:
        load.wait()

    width = gate_in.shape[0]
    identity = jnp.where(
        lax.broadcasted_iota(jnp.int32, (width, width), 0)
        == lax.broadcasted_iota(jnp.int32, (width, width), 1), 1.0, 0.0
    ).astype(jnp.bfloat16)

    @pl.loop(0, rows_in.shape[0] // 256)
    def _(tile):
        lines = columns_of(tile, 256)
        rows_now = rows_in[lines, :]
        pre_gate = dot_turned(rows_now, gate_in[...])
        pre_up = dot_turned(rows_now, up_in[...])
        hidden_grad = dot_turned(grads_in[lines, :], down_in[...])
        squash = jax.nn.sigmoid(pre_gate)
        hidden = (pre_gate * squash * pre_up).astype(jnp.bfloat16)
        gate_grad = (
            hidden_grad * pre_up * (squash * (1.0 + pre_gate * (1.0 - squash)))
        ).astype(jnp.bfloat16)
        up_grad = (hidden_grad * (pre_gate * squash)).astype(jnp.bfloat16)
        for value, plain, turned in (
            (hidden, hidden_in, hidden_turned_in),
            (gate_grad, gate_grad_in, gate_turned_in),
            (up_grad, up_grad_in, up_turned_in),
        ):
            plain[lines, :] = value
            turned[:, lines] = dot_turned(identity, value).astype(jnp.bfloat16)

    def make_weights(s):
        columns = columns_of(peer(s), depth)
        rows_now, grads_now = rows_in[:, columns], grads_in[:, columns]
        made[0, peer(s)] = dot(gate_turned_in[...], rows_now).astype(jnp.bfloat16)
        made[1, peer(s)] = dot(up_turned_in[...], rows_now).astype(jnp.bfloat16)
        made[2, peer(s)] = dot(hidden_turned_in[...], grads_now).astype(jnp.bfloat16)

    def make_parts(to):
        lines = columns_of(to, block)

        @pl.loop(0, features // 256)
        def _(tile):
            columns = columns_of(tile, 256)
            outs = dot(hidden_in[lines, :], down_in[:, columns])
            ins = dot(gate_grad_in[lines, :], gate_in[:, columns]) + dot(
                up_grad_in[lines, :], up_in[:, columns]
            )
            for e in range(ne):
                part[0, to, e, :, columns] = outs[e * cap : (e + 1) * cap].astype(jnp.bfloat16)
                part[1, to, e, :, columns] = ins[e * cap : (e + 1) * cap].astype(jnp.bfloat16)

    @pl.loop(1, ne)
    def _(s):
        make_weights(s)
        for k in range(3):
            weight_copy(k, s, me).start()

        @pl.when(s < nd)
        def _():
            make_parts(lax.rem(row + s, nd))

            @pl.loop(1, ne + 1)
            def _(step):
                for k in range(2):
                    fan_copy(k, lax.rem(step, ne), s).start()

    make_parts(row)
    make_weights(0)
    local = [
        pltpu.make_async_copy(made.at[k, me], weight_outs[k].at[me], local_sem.at[k])
        for k in range(3)
    ]
    for copy in local:
        copy.start()

    def add_up(s, target):
        for k in range(2):
            for r in range(1, nd):
                fan_copy(k, s, r).wait_recv()

            @pl.loop(0, features // 256)
            def _(tile):
                columns = columns_of(tile, 256)
                total = part[k, row, peer(s), :, columns].astype(jnp.float32)
                for r in range(1, nd):
                    total = total + arrived[k, r - 1, peer(s), :, columns].astype(jnp.float32)
                target[k, peer(s), :, columns] = total.astype(jnp.bfloat16)

    @pl.loop(1, ne)
    def _(s):
        add_up(s, summed)
        for k in range(2):
            home_copy(k, s, me).start()

    add_up(0, home)
    for copy in local:
        copy.wait()

    @pl.loop(0, ne)
    def _(s):
        for k in range(2):
            for r in range(1, nd):
                fan_copy(k, s, r).wait_send()

    @pl.loop(1, ne)
    def _(s):
        for k in range(2):
            home_copy(k, s, source(s)).wait()

    tok_rows = ids.shape[0]
    experts = lax.broadcasted_iota(jnp.int32, (tok_rows, 128), 1)
    named = [jnp.where(experts == ids[:, k : k + 1], 1.0, 0.0) for k in range(TOPK)]
    earlier = jnp.where(
        lax.broadcasted_iota(jnp.int32, (tok_rows, tok_rows), 0)
        > lax.broadcasted_iota(jnp.int32, (tok_rows, tok_rows), 1), 1.0, 0.0
    ).astype(jnp.bfloat16)
    place = dot(earlier, (named[0] + named[1]).astype(jnp.bfloat16)) + (experts * cap).astype(
        jnp.float32
    )
    places = lax.broadcasted_iota(jnp.int32, (tok_rows, block), 1).astype(jnp.float32)
    chosen = [
        jnp.where(places == jnp.sum(one * place, axis=1, keepdims=True), 1.0, 0.0)
        for one in named
    ]
    either = (chosen[0] + chosen[1]).astype(jnp.bfloat16)
    first, second = (one.astype(jnp.bfloat16) for one in chosen)
    first_scale, second_scale = scale[:, 0:1], scale[:, 1:2]

    def at_home(k, columns):
        return jnp.concatenate(
            [home[k, e, :, columns].astype(jnp.float32) for e in range(ne)], axis=0
        ).astype(jnp.bfloat16)

    @pl.loop(0, features // 256)
    def _(tile):
        columns = columns_of(tile, 256)
        outs = at_home(0, columns)
        mixed_out[:, columns] = (
            first_scale * dot(first, outs) + second_scale * dot(second, outs)
        ).astype(jnp.bfloat16)
        token_out[:, columns] = dot(either, at_home(1, columns)).astype(jnp.bfloat16)

    @pl.loop(1, ne)
    def _(s):
        for k in range(3):
            weight_copy(k, s, source(s)).wait()


def fused_combine(ne, nd, capacity, args, weight_type):
    rows, gate, ids = args[0], args[2], args[5]
    total, features = rows.shape
    width = gate.shape[0]
    anywhere, inside = pl.BlockSpec(memory_space=pl.ANY), pl.BlockSpec(memory_space=pltpu.VMEM)
    token_type = jax.ShapeDtypeStruct((ids.shape[0], features), jnp.bfloat16)
    dma = pltpu.SemaphoreType.DMA
    block = (ne, capacity, features)
    return pl.pallas_call(
        functools.partial(fused_combine_kernel, ne, nd),
        out_shape=[token_type] * 2 + [weight_type] * 3,
        in_specs=[anywhere] * 5 + [inside] * 2,
        out_specs=[inside] * 2 + [anywhere] * 3,
        scratch_shapes=[pltpu.VMEM(part.shape, part.dtype) for part in args[:5]] + [
            *([pltpu.VMEM((total, width), jnp.bfloat16)] * 3),
            *([pltpu.VMEM((width, total), jnp.bfloat16)] * 3),
            pltpu.VMEM((3,) + weight_type.shape, jnp.bfloat16),
            pltpu.VMEM((2, nd) + block, jnp.bfloat16),
            pltpu.VMEM((2, nd - 1) + block, jnp.bfloat16),
            pltpu.VMEM((2,) + block, jnp.bfloat16),
            pltpu.VMEM((2,) + block, jnp.bfloat16),
            dma((2, ne)), dma((2, ne)), dma((3, ne)), dma((3, ne)),
            dma((2, nd, ne)), dma((2, nd, ne)), dma((5,)), dma((3,)),
        ],
        compiler_params=pltpu.CompilerParams(
            collective_id=1, has_side_effects=True, vmem_limit_bytes=VMEM_BYTES
        ),
    )(*args)


def comm_call(kernel, ne, nd, args, out_shape, scratch, collective_id):
    anywhere = pl.BlockSpec(memory_space=pl.ANY)
    return pl.pallas_call(
        functools.partial(kernel, ne, nd),
        out_shape=out_shape,
        in_specs=[anywhere] * len(args),
        out_specs=[anywhere] * len(out_shape),
        scratch_shapes=scratch,
        compiler_params=pltpu.CompilerParams(
            collective_id=collective_id, has_side_effects=True, vmem_limit_bytes=VMEM_BYTES
        ),
    )(*args)


def shards(ne, nd, tokens, cotangent, expert_ids, gate_prob, gate_weight, up_weight, down_weight):
    experts, depth, width = gate_weight.shape
    tok_rows, features = tokens.shape
    pair_count = tok_rows * TOPK
    capacity = max(2, 5 * pair_count // (4 * experts))
    slots = experts * capacity
    if depth % 256 == 0 and capacity % 8 == 0 and width % 16 == 0 and nd * slots % 256 == 0:
        weights = tuple(part.transpose(0, 2, 1) for part in (gate_weight, up_weight, down_weight))
        rows, grads, *landed = fused_dispatch(
            ne, nd, capacity,
            (tokens, cotangent, expert_ids.T, gate_prob) + weights,
            jax.ShapeDtypeStruct((nd, experts, capacity, features), jnp.bfloat16),
            jax.ShapeDtypeStruct((width, features), jnp.bfloat16),
        )
        total = nd * slots
        mixed_out, grad_tokens, *weight_grads = fused_combine(
            ne, nd, capacity,
            (rows.reshape(total, features), grads.reshape(total, features), *landed,
             expert_ids, gate_prob),
            jax.ShapeDtypeStruct(weights[0].shape, jnp.bfloat16),
        )
        return (mixed_out, grad_tokens, *(part.transpose(0, 2, 1) for part in weight_grads))
    slot_of = slot_index(expert_ids, experts, capacity)
    gate_scale = gate_prob.reshape(-1)
    send_rows = (
        jnp.zeros((slots, features), jnp.bfloat16).at[slot_of].set(jnp.repeat(tokens, TOPK, axis=0))
    )
    scaled = (gate_scale[:, None] * jnp.repeat(cotangent, TOPK, axis=0).astype(jnp.float32)).astype(
        jnp.bfloat16
    )
    send_grads = jnp.zeros((slots, features), jnp.bfloat16).at[slot_of].set(scaled)
    slot_shape = (experts, capacity, features)
    dma = pltpu.SemaphoreType.DMA
    pair_type = jax.ShapeDtypeStruct((nd,) + slot_shape, jnp.bfloat16)
    home_type = jax.ShapeDtypeStruct(slot_shape, jnp.bfloat16)
    weight_type = jax.ShapeDtypeStruct(gate_weight.shape, jnp.bfloat16)
    rows, grads, gate, up, down = comm_call(
        dispatch_kernel, ne, nd,
        (send_rows.reshape(slot_shape), send_grads.reshape(slot_shape),
         gate_weight, up_weight, down_weight),
        [pair_type] * 2 + [weight_type] * 3,
        [dma((2, ne)), dma((2, ne)), dma((3, ne)), dma((3, ne)),
         dma((2, nd, ne)), dma((2, nd, ne)), dma((5,))],
        0,
    )
    total = nd * slots
    rows, grads = rows.reshape(total, features), grads.reshape(total, features)
    gate, up, down = (part.reshape(features, width) for part in (gate, up, down))
    contracted = (((0,), (0,)), ((), ()))
    turned = (((1,), (1,)), ((), ()))

    def dot_by(left, right, dims):
        return lax.dot_general(left, right, dims, preferred_element_type=jnp.float32)

    ahead = (((1,), (0,)), ((), ()))
    pre_gate = dot_by(rows, gate, ahead)
    pre_up = dot_by(rows, up, ahead)
    hidden_grad = dot_by(grads, down, ahead)
    squash = jax.nn.sigmoid(pre_gate)
    hidden = (pre_gate * squash * pre_up).astype(jnp.bfloat16)
    gate_grad = (hidden_grad * pre_up * (squash * (1.0 + pre_gate * (1.0 - squash)))).astype(
        jnp.bfloat16
    )
    up_grad = (hidden_grad * (pre_gate * squash)).astype(jnp.bfloat16)
    totals = tuple(
        dot_by(left, right, contracted).astype(jnp.bfloat16).reshape(gate_weight.shape)
        for left, right in ((rows, gate_grad), (rows, up_grad), (grads, hidden))
    )
    outputs = dot_by(hidden, down, turned).astype(jnp.bfloat16)
    input_grads = (dot_by(gate_grad, gate, turned) + dot_by(up_grad, up, turned)).astype(jnp.bfloat16)
    out_home, in_home, grad_gate, grad_up, grad_down = comm_call(
        combine_kernel, ne, nd,
        (outputs.reshape((nd,) + slot_shape), input_grads.reshape((nd,) + slot_shape)) + totals,
        [home_type] * 2 + [weight_type] * 3,
        [pltpu.VMEM((2,) + slot_shape, jnp.bfloat16),
         pltpu.VMEM((2, nd - 1) + slot_shape, jnp.bfloat16),
         pltpu.VMEM((2,) + slot_shape, jnp.bfloat16),
         dma((2, ne)), dma((2, ne)), dma((3, ne)), dma((3, ne)),
         dma((2, nd, ne)), dma((2, nd, ne)), dma((2, ne)), dma((5,))],
        1,
    )
    out_pairs = out_home.reshape(slots, features)[slot_of].astype(jnp.float32)
    mixed_out = jnp.sum(
        (gate_scale[:, None] * out_pairs).reshape(tok_rows, TOPK, features), axis=1
    ).astype(jnp.bfloat16)
    in_pairs = in_home.reshape(slots, features)[slot_of].astype(jnp.float32)
    grad_tokens = jnp.sum(in_pairs.reshape(tok_rows, TOPK, features), axis=1).astype(jnp.bfloat16)
    return (mixed_out, grad_tokens, grad_gate, grad_up, grad_down)


def solution(mesh):
    by_token = P(("dp", "expert"), None)
    by_block = P(None, "expert", "dp")
    return jax.shard_map(
        functools.partial(shards, mesh.shape["expert"], mesh.shape["dp"]),
        mesh=mesh,
        in_specs=(by_token,) * 4 + (by_block,) * 3,
        out_specs=(by_token,) * 2 + (by_block,) * 3,
        check_vma=False,
    )
```

```python
import functools

import jax
import jax.numpy as jnp
from jax import lax
from jax.experimental import pallas as pl
from jax.experimental.pallas import tpu as pltpu
from jax.sharding import PartitionSpec as P

TOPK = 2
VMEM_BYTES = 60 * 1024 * 1024


def slot_index(expert_ids, experts, capacity):
    flat_ids = expert_ids.reshape(-1)
    one_hot = (flat_ids[:, None] == jnp.arange(experts, dtype=jnp.int32)[None, :]).astype(jnp.int32)
    before = jnp.cumsum(one_hot, axis=0) - one_hot
    return flat_ids * capacity + jnp.sum(before * one_hot, axis=1)


def greet(ne, nd):
    me, row = lax.axis_index("expert"), lax.axis_index("dp")
    barrier = pltpu.get_barrier_semaphore()

    @pl.loop(1, ne)
    def _(s):
        pl.semaphore_signal(barrier, inc=1, device_id={"expert": lax.rem(me + s, ne)})

    @pl.loop(1, nd)
    def _(r):
        pl.semaphore_signal(barrier, inc=1, device_id={"dp": lax.rem(row + r, nd)})

    pl.semaphore_wait(barrier, ne - 1 + nd - 1)


def weight_slot(ref, landing):
    if len(ref.shape) == 3:
        return ref.at[landing]
    return ref.at[:, columns_of(landing, ref.shape[1] // lax.axis_size("expert"))]


def dot(left, right):
    return jnp.dot(left, right, preferred_element_type=jnp.float32)


def dot_turned(left, right):
    return lax.dot_general(
        left, right, (((1,), (1,)), ((), ())), preferred_element_type=jnp.float32
    )


def columns_of(index, size):
    return pl.ds(pl.multiple_of(index * size, size), size)


def dispatch_kernel(
    ne, nd,
    rows, grads, gate, up, down,
    rows_out, grads_out, gate_out, up_out, down_out,
    pair_send, pair_recv, weight_send, weight_recv, fan_send, fan_recv, local_sem,
):
    me, row = lax.axis_index("expert"), lax.axis_index("dp")
    pairs = ((rows, rows_out), (grads, grads_out))
    weights = ((gate, gate_out), (up, up_out), (down, down_out))

    def peer(s):
        return lax.rem(me + s, ne)

    def source(s):
        return lax.rem(me - s + ne, ne)

    def pair_copy(k, s, landing):
        return pltpu.make_async_remote_copy(
            src_ref=pairs[k][0].at[peer(s)], dst_ref=pairs[k][1].at[row, landing],
            send_sem=pair_send.at[k, s], recv_sem=pair_recv.at[k, s],
            device_id={"expert": peer(s)},
        )

    def weight_copy(k, s, landing):
        return pltpu.make_async_remote_copy(
            src_ref=weights[k][0].at[peer(s)], dst_ref=weight_slot(weights[k][1], landing),
            send_sem=weight_send.at[k, s], recv_sem=weight_recv.at[k, s],
            device_id={"expert": peer(s)},
        )

    def fan_copy(k, s, r, src, landing):
        return pltpu.make_async_remote_copy(
            src_ref=src, dst_ref=pairs[k][1].at[landing, source(s)],
            send_sem=fan_send.at[k, r, s], recv_sem=fan_recv.at[k, r, s],
            device_id={"dp": lax.rem(row + r, nd)},
        )

    greet(ne, nd)

    @pl.loop(1, ne)
    def _(s):
        for k in range(2):
            pair_copy(k, s, me).start()

    local = [
        pltpu.make_async_copy(pairs[k][0].at[me], pairs[k][1].at[row, me], local_sem.at[k])
        for k in range(2)
    ] + [
        pltpu.make_async_copy(
            weights[k][0].at[me], weight_slot(weights[k][1], me), local_sem.at[2 + k]
        )
        for k in range(3)
    ]
    for copy in local:
        copy.start()
    for k in range(2):
        for r in range(1, nd):
            fan_copy(k, 0, r, pairs[k][0].at[me], row).start()

    @pl.loop(1, ne)
    def _(s):
        for k in range(2):
            pair_copy(k, s, source(s)).wait_recv()
            for r in range(1, nd):
                fan_copy(k, s, r, pairs[k][1].at[row, source(s)], row).start()
        for k in range(3):
            weight_copy(k, s, me).start()

    for copy in local:
        copy.wait()

    @pl.loop(0, ne)
    def _(s):
        for k in range(2):
            for r in range(1, nd):
                arrived = fan_copy(
                    k, s, r, pairs[k][1].at[row, source(s)], lax.rem(row - r + nd, nd)
                )
                arrived.wait_send()
                arrived.wait_recv()

    @pl.loop(1, ne)
    def _(s):
        for k in range(2):
            pair_copy(k, s, me).wait_send()
        for k in range(3):
            weight_copy(k, s, source(s)).wait()


def fused_dispatch_kernel(
    ne, nd,
    tokens, cotangent, ids_turned, scale, gate, up, down,
    rows_out, grads_out, gate_out, up_out, down_out,
    rows, grads,
    pair_send, pair_recv, weight_send, weight_recv, fan_send, fan_recv, local_sem,
):
    me, row = lax.axis_index("expert"), lax.axis_index("dp")
    pairs = ((rows, rows_out), (grads, grads_out))
    weights = ((gate, gate_out), (up, up_out), (down, down_out))

    early = min(3, ne)

    def peer(s):
        return lax.rem(me + s, ne)

    def source(s):
        return lax.rem(me - s + ne, ne)

    def pair_copy(k, s, landing):
        return pltpu.make_async_remote_copy(
            src_ref=pairs[k][0].at[peer(s)], dst_ref=pairs[k][1].at[row, landing],
            send_sem=pair_send.at[k, s], recv_sem=pair_recv.at[k, s],
            device_id={"expert": peer(s)},
        )

    def weight_copy(k, s, landing):
        return pltpu.make_async_remote_copy(
            src_ref=weights[k][0].at[peer(s)], dst_ref=weight_slot(weights[k][1], landing),
            send_sem=weight_send.at[k, s], recv_sem=weight_recv.at[k, s],
            device_id={"expert": peer(s)},
        )

    def fan_copy(k, s, r, src, landing):
        return pltpu.make_async_remote_copy(
            src_ref=src, dst_ref=pairs[k][1].at[landing, source(s)],
            send_sem=fan_send.at[k, r, s], recv_sem=fan_recv.at[k, r, s],
            device_id={"dp": lax.rem(row + r, nd)},
        )

    greet(ne, nd)

    @pl.loop(1, early)
    def _(s):
        for k in range(3):
            weight_copy(k, s, me).start()

    cap, features = rows.shape[1:]
    tok_rows = tokens.shape[0]
    experts = lax.broadcasted_iota(jnp.int32, (ne, tok_rows), 0)
    named = [jnp.where(experts == ids_turned[k : k + 1, :], 1.0, 0.0) for k in range(TOPK)]
    earlier = jnp.where(
        lax.broadcasted_iota(jnp.int32, (tok_rows, tok_rows), 0)
        < lax.broadcasted_iota(jnp.int32, (tok_rows, tok_rows), 1), 1.0, 0.0
    ).astype(jnp.bfloat16)
    rank = dot((named[0] + named[1]).astype(jnp.bfloat16), earlier)
    place = rank + (experts * cap).astype(jnp.float32)
    slots = lax.broadcasted_iota(jnp.int32, (ne * cap, tok_rows), 0).astype(jnp.float32)
    first, second = (
        jnp.where(slots == jnp.sum(one * place, axis=0, keepdims=True), 1.0, 0.0) for one in named
    )
    either = (first + second).astype(jnp.bfloat16)
    first, second = first.astype(jnp.bfloat16), second.astype(jnp.bfloat16)

    @pl.loop(0, features // 256)
    def _(tile):
        columns = columns_of(tile, 256)
        cot = cotangent[:, columns].astype(jnp.float32)
        picked = dot(either, tokens[:, columns])
        picked_grads = dot(first, (scale[:, 0:1] * cot).astype(jnp.bfloat16)) + dot(
            second, (scale[:, 1:2] * cot).astype(jnp.bfloat16)
        )
        for e in range(ne):
            rows[e, :, columns] = picked[e * cap : (e + 1) * cap].astype(jnp.bfloat16)
            grads[e, :, columns] = picked_grads[e * cap : (e + 1) * cap].astype(jnp.bfloat16)

    @pl.loop(1, ne)
    def _(s):
        for k in range(2):
            pair_copy(k, s, me).start()

    local = [
        pltpu.make_async_copy(pairs[k][0].at[me], pairs[k][1].at[row, me], local_sem.at[k])
        for k in range(2)
    ] + [
        pltpu.make_async_copy(
            weights[k][0].at[me], weight_slot(weights[k][1], me), local_sem.at[2 + k]
        )
        for k in range(3)
    ]
    for copy in local:
        copy.start()
    for k in range(2):
        for r in range(1, nd):
            fan_copy(k, 0, r, pairs[k][0].at[me], row).start()

    @pl.loop(1, ne)
    def _(s):
        for k in range(2):
            pair_copy(k, s, source(s)).wait_recv()
            for r in range(1, nd):
                fan_copy(k, s, r, pairs[k][1].at[row, source(s)], row).start()
        @pl.when(s >= early)
        def _():
            for k in range(3):
                weight_copy(k, s, me).start()

    for copy in local:
        copy.wait()

    @pl.loop(0, ne)
    def _(s):
        for k in range(2):
            for r in range(1, nd):
                arrived = fan_copy(
                    k, s, r, pairs[k][1].at[row, source(s)], lax.rem(row - r + nd, nd)
                )
                arrived.wait_send()
                arrived.wait_recv()

    @pl.loop(1, ne)
    def _(s):
        for k in range(2):
            pair_copy(k, s, me).wait_send()
        for k in range(3):
            weight_copy(k, s, source(s)).wait()


def fused_dispatch(ne, nd, capacity, args, pair_type, landed_type):
    anywhere, inside = pl.BlockSpec(memory_space=pl.ANY), pl.BlockSpec(memory_space=pltpu.VMEM)
    dma = pltpu.SemaphoreType.DMA
    block = pair_type.shape[1:]
    return pl.pallas_call(
        functools.partial(fused_dispatch_kernel, ne, nd),
        out_shape=[pair_type] * 2 + [landed_type] * 3,
        in_specs=[inside] * 4 + [anywhere] * 3,
        out_specs=[anywhere] * 5,
        scratch_shapes=[
            pltpu.VMEM(block, jnp.bfloat16), pltpu.VMEM(block, jnp.bfloat16),
            dma((2, ne)), dma((2, ne)), dma((3, ne)), dma((3, ne)),
            dma((2, nd, ne)), dma((2, nd, ne)), dma((5,)),
        ],
        compiler_params=pltpu.CompilerParams(
            collective_id=2, has_side_effects=True, vmem_limit_bytes=VMEM_BYTES
        ),
    )(*args)


def combine_kernel(
    ne, nd,
    outs, ins, gate, up, down,
    outs_home, ins_home, gate_out, up_out, down_out,
    own, arrived, summed,
    home_send, home_recv, weight_send, weight_recv, fan_send, fan_recv, own_sem, local_sem,
):
    me, row = lax.axis_index("expert"), lax.axis_index("dp")
    parts = ((outs, outs_home), (ins, ins_home))
    weights = ((gate, gate_out), (up, up_out), (down, down_out))

    def peer(s):
        return lax.rem(me + s, ne)

    def source(s):
        return lax.rem(me - s + ne, ne)

    def home_copy(k, s, landing):
        return pltpu.make_async_remote_copy(
            src_ref=summed.at[k, peer(s)], dst_ref=parts[k][1].at[landing],
            send_sem=home_send.at[k, s], recv_sem=home_recv.at[k, s],
            device_id={"expert": peer(s)},
        )

    def weight_copy(k, s, landing):
        return pltpu.make_async_remote_copy(
            src_ref=weights[k][0].at[peer(s)], dst_ref=weights[k][1].at[landing],
            send_sem=weight_send.at[k, s], recv_sem=weight_recv.at[k, s],
            device_id={"expert": peer(s)},
        )

    def fan_copy(k, s, r):
        to = lax.rem(row + r, nd)
        return pltpu.make_async_remote_copy(
            src_ref=parts[k][0].at[to, peer(s)], dst_ref=arrived.at[k, r - 1, peer(s)],
            send_sem=fan_send.at[k, r, s], recv_sem=fan_recv.at[k, r, s],
            device_id={"dp": to},
        )

    def own_copy(k, s):
        return pltpu.make_async_copy(
            parts[k][0].at[row, peer(s)], own.at[k, peer(s)], own_sem.at[k, s]
        )

    greet(ne, nd)

    @pl.loop(1, ne)
    def _(s):
        for k in range(3):
            weight_copy(k, s, me).start()

    @pl.loop(1, ne + 1)
    def _(step):
        s = lax.rem(step, ne)
        for k in range(2):
            for r in range(1, nd):
                fan_copy(k, s, r).start()
            own_copy(k, s).start()

    local = [
        pltpu.make_async_copy(weights[k][0].at[me], weights[k][1].at[me], local_sem.at[k])
        for k in range(3)
    ]
    for copy in local:
        copy.start()

    def add_up(s):
        for k in range(2):
            own_copy(k, s).wait()
            total = own[k, peer(s)].astype(jnp.float32)
            for r in range(1, nd):
                fan_copy(k, s, r).wait_recv()
                total = total + arrived[k, r - 1, peer(s)].astype(jnp.float32)
            summed[k, peer(s)] = total.astype(jnp.bfloat16)

    @pl.loop(1, ne)
    def _(s):
        add_up(s)
        for k in range(2):
            home_copy(k, s, me).start()

    add_up(0)
    mine = [
        pltpu.make_async_copy(summed.at[k, me], parts[k][1].at[me], local_sem.at[3 + k])
        for k in range(2)
    ]
    for copy in mine:
        copy.start()
    for copy in local + mine:
        copy.wait()

    @pl.loop(0, ne)
    def _(s):
        for k in range(2):
            for r in range(1, nd):
                fan_copy(k, s, r).wait_send()

    @pl.loop(1, ne)
    def _(s):
        for k in range(2):
            home_copy(k, s, source(s)).wait()
        for k in range(3):
            weight_copy(k, s, source(s)).wait()


def fused_combine_kernel(
    ne, nd,
    rows, grads, gate, up, down, gate_grad, up_grad, hidden, gate_turned, up_turned, hidden_turned,
    ids, scale,
    mixed_out, token_out, gate_out, up_out, down_out,
    rows_in, grads_in, gate_in, up_in, down_in, gate_grad_in, up_grad_in, hidden_in,
    gate_turned_in, up_turned_in, hidden_turned_in,
    made, part, arrived, summed, home,
    home_send, home_recv, weight_send, weight_recv, fan_send, fan_recv, load_sem, local_sem,
):
    me, row = lax.axis_index("expert"), lax.axis_index("dp")
    weight_outs = (gate_out, up_out, down_out)
    features = rows.shape[1]
    depth = features // ne
    cap = part.shape[3]
    block = ne * cap

    def peer(s):
        return lax.rem(me + s, ne)

    def source(s):
        return lax.rem(me - s + ne, ne)

    def home_copy(k, s, landing):
        return pltpu.make_async_remote_copy(
            src_ref=summed.at[k, peer(s)], dst_ref=home.at[k, landing],
            send_sem=home_send.at[k, s], recv_sem=home_recv.at[k, s],
            device_id={"expert": peer(s)},
        )

    def weight_copy(k, s, landing):
        return pltpu.make_async_remote_copy(
            src_ref=made.at[k, peer(s)], dst_ref=weight_outs[k].at[landing],
            send_sem=weight_send.at[k, s], recv_sem=weight_recv.at[k, s],
            device_id={"expert": peer(s)},
        )

    def fan_copy(k, s, r):
        to = lax.rem(row + r, nd)
        return pltpu.make_async_remote_copy(
            src_ref=part.at[k, to, peer(s)], dst_ref=arrived.at[k, r - 1, peer(s)],
            send_sem=fan_send.at[k, r, s], recv_sem=fan_recv.at[k, r, s],
            device_id={"dp": to},
        )

    loads = [
        pltpu.make_async_copy(src, dst, load_sem.at[at])
        for at, (src, dst) in enumerate((
            (gate_turned, gate_turned_in), (rows, rows_in), (up_turned, up_turned_in),
            (hidden_turned, hidden_turned_in), (grads, grads_in),
            (hidden, hidden_in), (down, down_in), (gate_grad, gate_grad_in), (gate, gate_in),
            (up_grad, up_grad_in), (up, up_in),
        ))
    ]
    for load in loads:
        load.start()
    greet(ne, nd)
    for load in loads:
        load.wait()

    def make_weights(s):
        columns = columns_of(peer(s), depth)
        rows_now, grads_now = rows_in[:, columns], grads_in[:, columns]
        made[0, peer(s)] = dot(gate_turned_in[...], rows_now).astype(jnp.bfloat16)
        made[1, peer(s)] = dot(up_turned_in[...], rows_now).astype(jnp.bfloat16)
        made[2, peer(s)] = dot(hidden_turned_in[...], grads_now).astype(jnp.bfloat16)

    def make_parts(to):
        lines = columns_of(to, block)

        @pl.loop(0, features // 256)
        def _(tile):
            columns = columns_of(tile, 256)
            outs = dot(hidden_in[lines, :], down_in[:, columns])
            ins = dot(gate_grad_in[lines, :], gate_in[:, columns]) + dot(
                up_grad_in[lines, :], up_in[:, columns]
            )
            for e in range(ne):
                part[0, to, e, :, columns] = outs[e * cap : (e + 1) * cap].astype(jnp.bfloat16)
                part[1, to, e, :, columns] = ins[e * cap : (e + 1) * cap].astype(jnp.bfloat16)

    @pl.loop(1, ne)
    def _(s):
        make_weights(s)
        for k in range(3):
            weight_copy(k, s, me).start()

        @pl.when(s < nd)
        def _():
            make_parts(lax.rem(row + s, nd))

            @pl.loop(1, ne + 1)
            def _(step):
                for k in range(2):
                    fan_copy(k, lax.rem(step, ne), s).start()

    make_parts(row)
    make_weights(0)
    local = [
        pltpu.make_async_copy(made.at[k, me], weight_outs[k].at[me], local_sem.at[k])
        for k in range(3)
    ]
    for copy in local:
        copy.start()

    def add_up(s, target):
        for k in range(2):
            for r in range(1, nd):
                fan_copy(k, s, r).wait_recv()

            @pl.loop(0, features // 256)
            def _(tile):
                columns = columns_of(tile, 256)
                total = part[k, row, peer(s), :, columns].astype(jnp.float32)
                for r in range(1, nd):
                    total = total + arrived[k, r - 1, peer(s), :, columns].astype(jnp.float32)
                target[k, peer(s), :, columns] = total.astype(jnp.bfloat16)

    @pl.loop(1, ne)
    def _(s):
        add_up(s, summed)
        for k in range(2):
            home_copy(k, s, me).start()

    add_up(0, home)
    for copy in local:
        copy.wait()

    @pl.loop(0, ne)
    def _(s):
        for k in range(2):
            for r in range(1, nd):
                fan_copy(k, s, r).wait_send()

    @pl.loop(1, ne)
    def _(s):
        for k in range(2):
            home_copy(k, s, source(s)).wait()

    tok_rows = ids.shape[0]
    experts = lax.broadcasted_iota(jnp.int32, (tok_rows, 128), 1)
    named = [jnp.where(experts == ids[:, k : k + 1], 1.0, 0.0) for k in range(TOPK)]
    earlier = jnp.where(
        lax.broadcasted_iota(jnp.int32, (tok_rows, tok_rows), 0)
        > lax.broadcasted_iota(jnp.int32, (tok_rows, tok_rows), 1), 1.0, 0.0
    ).astype(jnp.bfloat16)
    place = dot(earlier, (named[0] + named[1]).astype(jnp.bfloat16)) + (experts * cap).astype(
        jnp.float32
    )
    places = lax.broadcasted_iota(jnp.int32, (tok_rows, block), 1).astype(jnp.float32)
    chosen = [
        jnp.where(places == jnp.sum(one * place, axis=1, keepdims=True), 1.0, 0.0)
        for one in named
    ]
    either = (chosen[0] + chosen[1]).astype(jnp.bfloat16)
    first, second = (one.astype(jnp.bfloat16) for one in chosen)
    first_scale, second_scale = scale[:, 0:1], scale[:, 1:2]

    def at_home(k, columns):
        return jnp.concatenate(
            [home[k, e, :, columns].astype(jnp.float32) for e in range(ne)], axis=0
        ).astype(jnp.bfloat16)

    @pl.loop(0, features // 256)
    def _(tile):
        columns = columns_of(tile, 256)
        outs = at_home(0, columns)
        mixed_out[:, columns] = (
            first_scale * dot(first, outs) + second_scale * dot(second, outs)
        ).astype(jnp.bfloat16)
        token_out[:, columns] = dot(either, at_home(1, columns)).astype(jnp.bfloat16)

    @pl.loop(1, ne)
    def _(s):
        for k in range(3):
            weight_copy(k, s, source(s)).wait()


def fused_combine(ne, nd, capacity, args, weight_type):
    rows, ids = args[0], args[11]
    features = rows.shape[1]
    anywhere, inside = pl.BlockSpec(memory_space=pl.ANY), pl.BlockSpec(memory_space=pltpu.VMEM)
    token_type = jax.ShapeDtypeStruct((ids.shape[0], features), jnp.bfloat16)
    dma = pltpu.SemaphoreType.DMA
    block = (ne, capacity, features)
    return pl.pallas_call(
        functools.partial(fused_combine_kernel, ne, nd),
        out_shape=[token_type] * 2 + [weight_type] * 3,
        in_specs=[anywhere] * 11 + [inside] * 2,
        out_specs=[inside] * 2 + [anywhere] * 3,
        scratch_shapes=[pltpu.VMEM(part.shape, part.dtype) for part in args[:11]] + [
            pltpu.VMEM((3,) + weight_type.shape, jnp.bfloat16),
            pltpu.VMEM((2, nd) + block, jnp.bfloat16),
            pltpu.VMEM((2, nd - 1) + block, jnp.bfloat16),
            pltpu.VMEM((2,) + block, jnp.bfloat16),
            pltpu.VMEM((2,) + block, jnp.bfloat16),
            dma((2, ne)), dma((2, ne)), dma((3, ne)), dma((3, ne)),
            dma((2, nd, ne)), dma((2, nd, ne)), dma((11,)), dma((3,)),
        ],
        compiler_params=pltpu.CompilerParams(
            collective_id=1, has_side_effects=True, vmem_limit_bytes=VMEM_BYTES
        ),
    )(*args)


def comm_call(kernel, ne, nd, args, out_shape, scratch, collective_id):
    anywhere = pl.BlockSpec(memory_space=pl.ANY)
    return pl.pallas_call(
        functools.partial(kernel, ne, nd),
        out_shape=out_shape,
        in_specs=[anywhere] * len(args),
        out_specs=[anywhere] * len(out_shape),
        scratch_shapes=scratch,
        compiler_params=pltpu.CompilerParams(
            collective_id=collective_id, has_side_effects=True, vmem_limit_bytes=VMEM_BYTES
        ),
    )(*args)


def shards(ne, nd, tokens, cotangent, expert_ids, gate_prob, gate_weight, up_weight, down_weight):
    experts, depth, width = gate_weight.shape
    tok_rows, features = tokens.shape
    pair_count = tok_rows * TOPK
    capacity = max(2, 5 * pair_count // (4 * experts))
    slots = experts * capacity
    if depth % 256 == 0 and capacity % 8 == 0 and width % 16 == 0 and nd * slots % 256 == 0:
        weights = tuple(part.transpose(0, 2, 1) for part in (gate_weight, up_weight, down_weight))
        rows, grads, *landed = fused_dispatch(
            ne, nd, capacity,
            (tokens, cotangent, expert_ids.T, gate_prob) + weights,
            jax.ShapeDtypeStruct((nd, experts, capacity, features), jnp.bfloat16),
            jax.ShapeDtypeStruct((width, features), jnp.bfloat16),
        )
        total = nd * slots
        rows, grads = rows.reshape(total, features), grads.reshape(total, features)
        gate, up, down = landed
        pre_gate = dot_turned(rows, gate)
        pre_up = dot_turned(rows, up)
        hidden_grad = dot_turned(grads, down)
        squash = jax.nn.sigmoid(pre_gate)
        hidden = (pre_gate * squash * pre_up).astype(jnp.bfloat16)
        gate_grad = (
            hidden_grad * pre_up * (squash * (1.0 + pre_gate * (1.0 - squash)))
        ).astype(jnp.bfloat16)
        up_grad = (hidden_grad * (pre_gate * squash)).astype(jnp.bfloat16)
        mixed_out, grad_tokens, *weight_grads = fused_combine(
            ne, nd, capacity,
            (rows, grads, gate, up, down, gate_grad, up_grad, hidden,
             gate_grad.T, up_grad.T, hidden.T, expert_ids, gate_prob),
            jax.ShapeDtypeStruct(weights[0].shape, jnp.bfloat16),
        )
        return (mixed_out, grad_tokens, *(part.transpose(0, 2, 1) for part in weight_grads))
    slot_of = slot_index(expert_ids, experts, capacity)
    gate_scale = gate_prob.reshape(-1)
    send_rows = (
        jnp.zeros((slots, features), jnp.bfloat16).at[slot_of].set(jnp.repeat(tokens, TOPK, axis=0))
    )
    scaled = (gate_scale[:, None] * jnp.repeat(cotangent, TOPK, axis=0).astype(jnp.float32)).astype(
        jnp.bfloat16
    )
    send_grads = jnp.zeros((slots, features), jnp.bfloat16).at[slot_of].set(scaled)
    slot_shape = (experts, capacity, features)
    dma = pltpu.SemaphoreType.DMA
    pair_type = jax.ShapeDtypeStruct((nd,) + slot_shape, jnp.bfloat16)
    home_type = jax.ShapeDtypeStruct(slot_shape, jnp.bfloat16)
    weight_type = jax.ShapeDtypeStruct(gate_weight.shape, jnp.bfloat16)
    rows, grads, gate, up, down = comm_call(
        dispatch_kernel, ne, nd,
        (send_rows.reshape(slot_shape), send_grads.reshape(slot_shape),
         gate_weight, up_weight, down_weight),
        [pair_type] * 2 + [weight_type] * 3,
        [dma((2, ne)), dma((2, ne)), dma((3, ne)), dma((3, ne)),
         dma((2, nd, ne)), dma((2, nd, ne)), dma((5,))],
        0,
    )
    total = nd * slots
    rows, grads = rows.reshape(total, features), grads.reshape(total, features)
    gate, up, down = (part.reshape(features, width) for part in (gate, up, down))
    contracted = (((0,), (0,)), ((), ()))
    turned = (((1,), (1,)), ((), ()))

    def dot_by(left, right, dims):
        return lax.dot_general(left, right, dims, preferred_element_type=jnp.float32)

    ahead = (((1,), (0,)), ((), ()))
    pre_gate = dot_by(rows, gate, ahead)
    pre_up = dot_by(rows, up, ahead)
    hidden_grad = dot_by(grads, down, ahead)
    squash = jax.nn.sigmoid(pre_gate)
    hidden = (pre_gate * squash * pre_up).astype(jnp.bfloat16)
    gate_grad = (hidden_grad * pre_up * (squash * (1.0 + pre_gate * (1.0 - squash)))).astype(
        jnp.bfloat16
    )
    up_grad = (hidden_grad * (pre_gate * squash)).astype(jnp.bfloat16)
    totals = tuple(
        dot_by(left, right, contracted).astype(jnp.bfloat16).reshape(gate_weight.shape)
        for left, right in ((rows, gate_grad), (rows, up_grad), (grads, hidden))
    )
    outputs = dot_by(hidden, down, turned).astype(jnp.bfloat16)
    input_grads = (dot_by(gate_grad, gate, turned) + dot_by(up_grad, up, turned)).astype(jnp.bfloat16)
    out_home, in_home, grad_gate, grad_up, grad_down = comm_call(
        combine_kernel, ne, nd,
        (outputs.reshape((nd,) + slot_shape), input_grads.reshape((nd,) + slot_shape)) + totals,
        [home_type] * 2 + [weight_type] * 3,
        [pltpu.VMEM((2,) + slot_shape, jnp.bfloat16),
         pltpu.VMEM((2, nd - 1) + slot_shape, jnp.bfloat16),
         pltpu.VMEM((2,) + slot_shape, jnp.bfloat16),
         dma((2, ne)), dma((2, ne)), dma((3, ne)), dma((3, ne)),
         dma((2, nd, ne)), dma((2, nd, ne)), dma((2, ne)), dma((5,))],
        1,
    )
    out_pairs = out_home.reshape(slots, features)[slot_of].astype(jnp.float32)
    mixed_out = jnp.sum(
        (gate_scale[:, None] * out_pairs).reshape(tok_rows, TOPK, features), axis=1
    ).astype(jnp.bfloat16)
    in_pairs = in_home.reshape(slots, features)[slot_of].astype(jnp.float32)
    grad_tokens = jnp.sum(in_pairs.reshape(tok_rows, TOPK, features), axis=1).astype(jnp.bfloat16)
    return (mixed_out, grad_tokens, grad_gate, grad_up, grad_down)


def solution(mesh):
    by_token = P(("dp", "expert"), None)
    by_block = P(None, "expert", "dp")
    return jax.shard_map(
        functools.partial(shards, mesh.shape["expert"], mesh.shape["dp"]),
        mesh=mesh,
        in_specs=(by_token,) * 4 + (by_block,) * 3,
        out_specs=(by_token,) * 2 + (by_block,) * 3,
        check_vma=False,
    )
```

```python
import functools

import jax
import jax.numpy as jnp
from jax import lax
from jax.experimental import pallas as pl
from jax.experimental.pallas import tpu as pltpu
from jax.sharding import PartitionSpec as P

TOPK = 2
VMEM_BYTES = 60 * 1024 * 1024


def slot_index(expert_ids, experts, capacity):
    flat_ids = expert_ids.reshape(-1)
    one_hot = (flat_ids[:, None] == jnp.arange(experts, dtype=jnp.int32)[None, :]).astype(jnp.int32)
    before = jnp.cumsum(one_hot, axis=0) - one_hot
    return flat_ids * capacity + jnp.sum(before * one_hot, axis=1)


def greet(ne, nd):
    me, row = lax.axis_index("expert"), lax.axis_index("dp")
    barrier = pltpu.get_barrier_semaphore()

    @pl.loop(1, ne)
    def _(s):
        pl.semaphore_signal(barrier, inc=1, device_id={"expert": lax.rem(me + s, ne)})

    @pl.loop(1, nd)
    def _(r):
        pl.semaphore_signal(barrier, inc=1, device_id={"dp": lax.rem(row + r, nd)})

    pl.semaphore_wait(barrier, ne - 1 + nd - 1)


def weight_slot(ref, landing):
    if len(ref.shape) == 3:
        return ref.at[landing]
    return ref.at[:, columns_of(landing, ref.shape[1] // lax.axis_size("expert"))]


def dot(left, right):
    return jnp.dot(left, right, preferred_element_type=jnp.float32)


def dot_turned(left, right):
    return lax.dot_general(
        left, right, (((1,), (1,)), ((), ())), preferred_element_type=jnp.float32
    )


def columns_of(index, size):
    return pl.ds(pl.multiple_of(index * size, size), size)


def dispatch_kernel(
    ne, nd,
    rows, grads, gate, up, down,
    rows_out, grads_out, gate_out, up_out, down_out,
    pair_send, pair_recv, weight_send, weight_recv, fan_send, fan_recv, local_sem,
):
    me, row = lax.axis_index("expert"), lax.axis_index("dp")
    pairs = ((rows, rows_out), (grads, grads_out))
    weights = ((gate, gate_out), (up, up_out), (down, down_out))

    def peer(s):
        return lax.rem(me + s, ne)

    def source(s):
        return lax.rem(me - s + ne, ne)

    def pair_copy(k, s, landing):
        return pltpu.make_async_remote_copy(
            src_ref=pairs[k][0].at[peer(s)], dst_ref=pairs[k][1].at[row, landing],
            send_sem=pair_send.at[k, s], recv_sem=pair_recv.at[k, s],
            device_id={"expert": peer(s)},
        )

    def weight_copy(k, s, landing):
        return pltpu.make_async_remote_copy(
            src_ref=weights[k][0].at[peer(s)], dst_ref=weight_slot(weights[k][1], landing),
            send_sem=weight_send.at[k, s], recv_sem=weight_recv.at[k, s],
            device_id={"expert": peer(s)},
        )

    def fan_copy(k, s, r, src, landing):
        return pltpu.make_async_remote_copy(
            src_ref=src, dst_ref=pairs[k][1].at[landing, source(s)],
            send_sem=fan_send.at[k, r, s], recv_sem=fan_recv.at[k, r, s],
            device_id={"dp": lax.rem(row + r, nd)},
        )

    greet(ne, nd)

    @pl.loop(1, ne)
    def _(s):
        for k in range(2):
            pair_copy(k, s, me).start()

    local = [
        pltpu.make_async_copy(pairs[k][0].at[me], pairs[k][1].at[row, me], local_sem.at[k])
        for k in range(2)
    ] + [
        pltpu.make_async_copy(
            weights[k][0].at[me], weight_slot(weights[k][1], me), local_sem.at[2 + k]
        )
        for k in range(3)
    ]
    for copy in local:
        copy.start()
    for k in range(2):
        for r in range(1, nd):
            fan_copy(k, 0, r, pairs[k][0].at[me], row).start()

    @pl.loop(1, ne)
    def _(s):
        for k in range(2):
            pair_copy(k, s, source(s)).wait_recv()
            for r in range(1, nd):
                fan_copy(k, s, r, pairs[k][1].at[row, source(s)], row).start()
        for k in range(3):
            weight_copy(k, s, me).start()

    for copy in local:
        copy.wait()

    @pl.loop(0, ne)
    def _(s):
        for k in range(2):
            for r in range(1, nd):
                arrived = fan_copy(
                    k, s, r, pairs[k][1].at[row, source(s)], lax.rem(row - r + nd, nd)
                )
                arrived.wait_send()
                arrived.wait_recv()

    @pl.loop(1, ne)
    def _(s):
        for k in range(2):
            pair_copy(k, s, me).wait_send()
        for k in range(3):
            weight_copy(k, s, source(s)).wait()


def fused_dispatch_kernel(
    ne, nd,
    tokens, cotangent, ids_turned, scale, gate, up, down,
    rows_out, grads_out, gate_out, up_out, down_out,
    rows, grads,
    pair_send, pair_recv, weight_send, weight_recv, fan_send, fan_recv, local_sem,
):
    me, row = lax.axis_index("expert"), lax.axis_index("dp")
    pairs = ((rows, rows_out), (grads, grads_out))
    weights = ((gate, gate_out), (up, up_out), (down, down_out))

    early = 1

    def peer(s):
        return lax.rem(me + s, ne)

    def source(s):
        return lax.rem(me - s + ne, ne)

    def pair_copy(k, s, landing):
        return pltpu.make_async_remote_copy(
            src_ref=pairs[k][0].at[peer(s)], dst_ref=pairs[k][1].at[row, landing],
            send_sem=pair_send.at[k, s], recv_sem=pair_recv.at[k, s],
            device_id={"expert": peer(s)},
        )

    def weight_copy(k, s, landing):
        return pltpu.make_async_remote_copy(
            src_ref=weights[k][0].at[peer(s)], dst_ref=weight_slot(weights[k][1], landing),
            send_sem=weight_send.at[k, s], recv_sem=weight_recv.at[k, s],
            device_id={"expert": peer(s)},
        )

    def fan_copy(k, s, r, src, landing):
        return pltpu.make_async_remote_copy(
            src_ref=src, dst_ref=pairs[k][1].at[landing, source(s)],
            send_sem=fan_send.at[k, r, s], recv_sem=fan_recv.at[k, r, s],
            device_id={"dp": lax.rem(row + r, nd)},
        )

    greet(ne, nd)

    @pl.loop(1, early)
    def _(s):
        for k in range(3):
            weight_copy(k, s, me).start()

    cap, features = rows.shape[1:]
    tok_rows = tokens.shape[0]
    experts = lax.broadcasted_iota(jnp.int32, (ne, tok_rows), 0)
    named = [jnp.where(experts == ids_turned[k : k + 1, :], 1.0, 0.0) for k in range(TOPK)]
    earlier = jnp.where(
        lax.broadcasted_iota(jnp.int32, (tok_rows, tok_rows), 0)
        < lax.broadcasted_iota(jnp.int32, (tok_rows, tok_rows), 1), 1.0, 0.0
    ).astype(jnp.bfloat16)
    rank = dot((named[0] + named[1]).astype(jnp.bfloat16), earlier)
    place = rank + (experts * cap).astype(jnp.float32)
    slots = lax.broadcasted_iota(jnp.int32, (ne * cap, tok_rows), 0).astype(jnp.float32)
    first, second = (
        jnp.where(slots == jnp.sum(one * place, axis=0, keepdims=True), 1.0, 0.0) for one in named
    )
    either = (first + second).astype(jnp.bfloat16)
    first, second = first.astype(jnp.bfloat16), second.astype(jnp.bfloat16)

    @pl.loop(0, features // 256)
    def _(tile):
        columns = columns_of(tile, 256)
        cot = cotangent[:, columns].astype(jnp.float32)
        picked = dot(either, tokens[:, columns])
        picked_grads = dot(first, (scale[:, 0:1] * cot).astype(jnp.bfloat16)) + dot(
            second, (scale[:, 1:2] * cot).astype(jnp.bfloat16)
        )
        for e in range(ne):
            rows[e, :, columns] = picked[e * cap : (e + 1) * cap].astype(jnp.bfloat16)
            grads[e, :, columns] = picked_grads[e * cap : (e + 1) * cap].astype(jnp.bfloat16)

    @pl.loop(1, ne)
    def _(s):
        for k in range(2):
            pair_copy(k, s, me).start()

    local = [
        pltpu.make_async_copy(pairs[k][0].at[me], pairs[k][1].at[row, me], local_sem.at[k])
        for k in range(2)
    ] + [
        pltpu.make_async_copy(
            weights[k][0].at[me], weight_slot(weights[k][1], me), local_sem.at[2 + k]
        )
        for k in range(3)
    ]
    for copy in local:
        copy.start()
    for k in range(2):
        for r in range(1, nd):
            fan_copy(k, 0, r, pairs[k][0].at[me], row).start()

    @pl.loop(1, ne)
    def _(s):
        for k in range(2):
            pair_copy(k, s, source(s)).wait_recv()
            for r in range(1, nd):
                fan_copy(k, s, r, pairs[k][1].at[row, source(s)], row).start()
        @pl.when(s >= early)
        def _():
            for k in range(3):
                weight_copy(k, s, me).start()

    for copy in local:
        copy.wait()

    @pl.loop(0, ne)
    def _(s):
        for k in range(2):
            for r in range(1, nd):
                arrived = fan_copy(
                    k, s, r, pairs[k][1].at[row, source(s)], lax.rem(row - r + nd, nd)
                )
                arrived.wait_send()
                arrived.wait_recv()

    @pl.loop(1, ne)
    def _(s):
        for k in range(2):
            pair_copy(k, s, me).wait_send()
        for k in range(3):
            weight_copy(k, s, source(s)).wait()


def fused_dispatch(ne, nd, capacity, args, pair_type, landed_type):
    anywhere, inside = pl.BlockSpec(memory_space=pl.ANY), pl.BlockSpec(memory_space=pltpu.VMEM)
    dma = pltpu.SemaphoreType.DMA
    block = pair_type.shape[1:]
    return pl.pallas_call(
        functools.partial(fused_dispatch_kernel, ne, nd),
        out_shape=[pair_type] * 2 + [landed_type] * 3,
        in_specs=[inside] * 4 + [anywhere] * 3,
        out_specs=[anywhere] * 5,
        scratch_shapes=[
            pltpu.VMEM(block, jnp.bfloat16), pltpu.VMEM(block, jnp.bfloat16),
            dma((2, ne)), dma((2, ne)), dma((3, ne)), dma((3, ne)),
            dma((2, nd, ne)), dma((2, nd, ne)), dma((5,)),
        ],
        compiler_params=pltpu.CompilerParams(
            collective_id=2, has_side_effects=True, vmem_limit_bytes=VMEM_BYTES
        ),
    )(*args)


def combine_kernel(
    ne, nd,
    outs, ins, gate, up, down,
    outs_home, ins_home, gate_out, up_out, down_out,
    own, arrived, summed,
    home_send, home_recv, weight_send, weight_recv, fan_send, fan_recv, own_sem, local_sem,
):
    me, row = lax.axis_index("expert"), lax.axis_index("dp")
    parts = ((outs, outs_home), (ins, ins_home))
    weights = ((gate, gate_out), (up, up_out), (down, down_out))

    def peer(s):
        return lax.rem(me + s, ne)

    def source(s):
        return lax.rem(me - s + ne, ne)

    def home_copy(k, s, landing):
        return pltpu.make_async_remote_copy(
            src_ref=summed.at[k, peer(s)], dst_ref=parts[k][1].at[landing],
            send_sem=home_send.at[k, s], recv_sem=home_recv.at[k, s],
            device_id={"expert": peer(s)},
        )

    def weight_copy(k, s, landing):
        return pltpu.make_async_remote_copy(
            src_ref=weights[k][0].at[peer(s)], dst_ref=weights[k][1].at[landing],
            send_sem=weight_send.at[k, s], recv_sem=weight_recv.at[k, s],
            device_id={"expert": peer(s)},
        )

    def fan_copy(k, s, r):
        to = lax.rem(row + r, nd)
        return pltpu.make_async_remote_copy(
            src_ref=parts[k][0].at[to, peer(s)], dst_ref=arrived.at[k, r - 1, peer(s)],
            send_sem=fan_send.at[k, r, s], recv_sem=fan_recv.at[k, r, s],
            device_id={"dp": to},
        )

    def own_copy(k, s):
        return pltpu.make_async_copy(
            parts[k][0].at[row, peer(s)], own.at[k, peer(s)], own_sem.at[k, s]
        )

    greet(ne, nd)

    @pl.loop(1, ne)
    def _(s):
        for k in range(3):
            weight_copy(k, s, me).start()

    @pl.loop(1, ne + 1)
    def _(step):
        s = lax.rem(step, ne)
        for k in range(2):
            for r in range(1, nd):
                fan_copy(k, s, r).start()
            own_copy(k, s).start()

    local = [
        pltpu.make_async_copy(weights[k][0].at[me], weights[k][1].at[me], local_sem.at[k])
        for k in range(3)
    ]
    for copy in local:
        copy.start()

    def add_up(s):
        for k in range(2):
            own_copy(k, s).wait()
            total = own[k, peer(s)].astype(jnp.float32)
            for r in range(1, nd):
                fan_copy(k, s, r).wait_recv()
                total = total + arrived[k, r - 1, peer(s)].astype(jnp.float32)
            summed[k, peer(s)] = total.astype(jnp.bfloat16)

    @pl.loop(1, ne)
    def _(s):
        add_up(s)
        for k in range(2):
            home_copy(k, s, me).start()

    add_up(0)
    mine = [
        pltpu.make_async_copy(summed.at[k, me], parts[k][1].at[me], local_sem.at[3 + k])
        for k in range(2)
    ]
    for copy in mine:
        copy.start()
    for copy in local + mine:
        copy.wait()

    @pl.loop(0, ne)
    def _(s):
        for k in range(2):
            for r in range(1, nd):
                fan_copy(k, s, r).wait_send()

    @pl.loop(1, ne)
    def _(s):
        for k in range(2):
            home_copy(k, s, source(s)).wait()
        for k in range(3):
            weight_copy(k, s, source(s)).wait()


def fused_combine_kernel(
    ne, nd,
    rows, grads, gate, up, down, ids, scale,
    mixed_out, token_out, gate_out, up_out, down_out,
    rows_in, grads_in, gate_in, up_in, down_in, gate_grad_in, up_grad_in, hidden_in,
    gate_turned_in, up_turned_in, hidden_turned_in,
    made, part, arrived, summed, home,
    home_send, home_recv, weight_send, weight_recv, fan_send, fan_recv, load_sem, local_sem,
):
    me, row = lax.axis_index("expert"), lax.axis_index("dp")
    weight_outs = (gate_out, up_out, down_out)
    features = rows.shape[1]
    depth = features // ne
    cap = part.shape[3]
    block = ne * cap

    def peer(s):
        return lax.rem(me + s, ne)

    def source(s):
        return lax.rem(me - s + ne, ne)

    def home_copy(k, s, landing):
        return pltpu.make_async_remote_copy(
            src_ref=summed.at[k, peer(s)], dst_ref=home.at[k, landing],
            send_sem=home_send.at[k, s], recv_sem=home_recv.at[k, s],
            device_id={"expert": peer(s)},
        )

    def weight_copy(k, s, landing):
        return pltpu.make_async_remote_copy(
            src_ref=made.at[k, peer(s)], dst_ref=weight_outs[k].at[landing],
            send_sem=weight_send.at[k, s], recv_sem=weight_recv.at[k, s],
            device_id={"expert": peer(s)},
        )

    def fan_copy(k, s, r):
        to = lax.rem(row + r, nd)
        return pltpu.make_async_remote_copy(
            src_ref=part.at[k, to, peer(s)], dst_ref=arrived.at[k, r - 1, peer(s)],
            send_sem=fan_send.at[k, r, s], recv_sem=fan_recv.at[k, r, s],
            device_id={"dp": to},
        )

    loads = [
        pltpu.make_async_copy(src, dst, load_sem.at[at])
        for at, (src, dst) in enumerate((
            (gate, gate_in), (up, up_in), (down, down_in), (rows, rows_in), (grads, grads_in),
        ))
    ]
    for load in loads:
        load.start()
    greet(ne, nd)
    for load in loads:
        load.wait()

    width = gate_in.shape[0]
    identity = jnp.where(
        lax.broadcasted_iota(jnp.int32, (width, width), 0)
        == lax.broadcasted_iota(jnp.int32, (width, width), 1), 1.0, 0.0
    ).astype(jnp.bfloat16)

    @pl.loop(0, rows_in.shape[0] // 256)
    def _(tile):
        lines = columns_of(tile, 256)
        rows_now = rows_in[lines, :]
        pre_gate = dot_turned(rows_now, gate_in[...])
        pre_up = dot_turned(rows_now, up_in[...])
        hidden_grad = dot_turned(grads_in[lines, :], down_in[...])
        squash = jax.nn.sigmoid(pre_gate)
        hidden = (pre_gate * squash * pre_up).astype(jnp.bfloat16)
        gate_grad = (
            hidden_grad * pre_up * (squash * (1.0 + pre_gate * (1.0 - squash)))
        ).astype(jnp.bfloat16)
        up_grad = (hidden_grad * (pre_gate * squash)).astype(jnp.bfloat16)
        for value, plain, turned in (
            (hidden, hidden_in, hidden_turned_in),
            (gate_grad, gate_grad_in, gate_turned_in),
            (up_grad, up_grad_in, up_turned_in),
        ):
            plain[lines, :] = value
            turned[:, lines] = dot_turned(identity, value).astype(jnp.bfloat16)

    def make_weights(s):
        columns = columns_of(peer(s), depth)
        rows_now, grads_now = rows_in[:, columns], grads_in[:, columns]
        made[0, peer(s)] = dot(gate_turned_in[...], rows_now).astype(jnp.bfloat16)
        made[1, peer(s)] = dot(up_turned_in[...], rows_now).astype(jnp.bfloat16)
        made[2, peer(s)] = dot(hidden_turned_in[...], grads_now).astype(jnp.bfloat16)

    def make_parts(to):
        lines = columns_of(to, block)

        @pl.loop(0, features // 256)
        def _(tile):
            columns = columns_of(tile, 256)
            outs = dot(hidden_in[lines, :], down_in[:, columns])
            ins = dot(gate_grad_in[lines, :], gate_in[:, columns]) + dot(
                up_grad_in[lines, :], up_in[:, columns]
            )
            for e in range(ne):
                part[0, to, e, :, columns] = outs[e * cap : (e + 1) * cap].astype(jnp.bfloat16)
                part[1, to, e, :, columns] = ins[e * cap : (e + 1) * cap].astype(jnp.bfloat16)

    @pl.loop(1, ne)
    def _(s):
        make_weights(s)
        for k in range(3):
            weight_copy(k, s, me).start()

        @pl.when(s < nd)
        def _():
            make_parts(lax.rem(row + s, nd))

            @pl.loop(1, ne + 1)
            def _(step):
                for k in range(2):
                    fan_copy(k, lax.rem(step, ne), s).start()

    make_parts(row)
    make_weights(0)
    local = [
        pltpu.make_async_copy(made.at[k, me], weight_outs[k].at[me], local_sem.at[k])
        for k in range(3)
    ]
    for copy in local:
        copy.start()

    def add_up(s, target):
        for k in range(2):
            for r in range(1, nd):
                fan_copy(k, s, r).wait_recv()

            @pl.loop(0, features // 256)
            def _(tile):
                columns = columns_of(tile, 256)
                total = part[k, row, peer(s), :, columns].astype(jnp.float32)
                for r in range(1, nd):
                    total = total + arrived[k, r - 1, peer(s), :, columns].astype(jnp.float32)
                target[k, peer(s), :, columns] = total.astype(jnp.bfloat16)

    @pl.loop(1, ne)
    def _(s):
        add_up(s, summed)
        for k in range(2):
            home_copy(k, s, me).start()

    add_up(0, home)
    for copy in local:
        copy.wait()

    @pl.loop(0, ne)
    def _(s):
        for k in range(2):
            for r in range(1, nd):
                fan_copy(k, s, r).wait_send()

    @pl.loop(1, ne)
    def _(s):
        for k in range(2):
            home_copy(k, s, source(s)).wait()

    tok_rows = ids.shape[0]
    experts = lax.broadcasted_iota(jnp.int32, (tok_rows, 128), 1)
    named = [jnp.where(experts == ids[:, k : k + 1], 1.0, 0.0) for k in range(TOPK)]
    earlier = jnp.where(
        lax.broadcasted_iota(jnp.int32, (tok_rows, tok_rows), 0)
        > lax.broadcasted_iota(jnp.int32, (tok_rows, tok_rows), 1), 1.0, 0.0
    ).astype(jnp.bfloat16)
    place = dot(earlier, (named[0] + named[1]).astype(jnp.bfloat16)) + (experts * cap).astype(
        jnp.float32
    )
    places = lax.broadcasted_iota(jnp.int32, (tok_rows, block), 1).astype(jnp.float32)
    chosen = [
        jnp.where(places == jnp.sum(one * place, axis=1, keepdims=True), 1.0, 0.0)
        for one in named
    ]
    either = (chosen[0] + chosen[1]).astype(jnp.bfloat16)
    first, second = (one.astype(jnp.bfloat16) for one in chosen)
    first_scale, second_scale = scale[:, 0:1], scale[:, 1:2]

    def at_home(k, columns):
        return jnp.concatenate(
            [home[k, e, :, columns].astype(jnp.float32) for e in range(ne)], axis=0
        ).astype(jnp.bfloat16)

    @pl.loop(0, features // 256)
    def _(tile):
        columns = columns_of(tile, 256)
        outs = at_home(0, columns)
        mixed_out[:, columns] = (
            first_scale * dot(first, outs) + second_scale * dot(second, outs)
        ).astype(jnp.bfloat16)
        token_out[:, columns] = dot(either, at_home(1, columns)).astype(jnp.bfloat16)

    @pl.loop(1, ne)
    def _(s):
        for k in range(3):
            weight_copy(k, s, source(s)).wait()


def fused_combine(ne, nd, capacity, args, weight_type):
    rows, gate, ids = args[0], args[2], args[5]
    total, features = rows.shape
    width = gate.shape[0]
    anywhere, inside = pl.BlockSpec(memory_space=pl.ANY), pl.BlockSpec(memory_space=pltpu.VMEM)
    token_type = jax.ShapeDtypeStruct((ids.shape[0], features), jnp.bfloat16)
    dma = pltpu.SemaphoreType.DMA
    block = (ne, capacity, features)
    return pl.pallas_call(
        functools.partial(fused_combine_kernel, ne, nd),
        out_shape=[token_type] * 2 + [weight_type] * 3,
        in_specs=[anywhere] * 5 + [inside] * 2,
        out_specs=[inside] * 2 + [anywhere] * 3,
        scratch_shapes=[pltpu.VMEM(part.shape, part.dtype) for part in args[:5]] + [
            *([pltpu.VMEM((total, width), jnp.bfloat16)] * 3),
            *([pltpu.VMEM((width, total), jnp.bfloat16)] * 3),
            pltpu.VMEM((3,) + weight_type.shape, jnp.bfloat16),
            pltpu.VMEM((2, nd) + block, jnp.bfloat16),
            pltpu.VMEM((2, nd - 1) + block, jnp.bfloat16),
            pltpu.VMEM((2,) + block, jnp.bfloat16),
            pltpu.VMEM((2,) + block, jnp.bfloat16),
            dma((2, ne)), dma((2, ne)), dma((3, ne)), dma((3, ne)),
            dma((2, nd, ne)), dma((2, nd, ne)), dma((5,)), dma((3,)),
        ],
        compiler_params=pltpu.CompilerParams(
            collective_id=1, has_side_effects=True, vmem_limit_bytes=VMEM_BYTES
        ),
    )(*args)


def comm_call(kernel, ne, nd, args, out_shape, scratch, collective_id):
    anywhere = pl.BlockSpec(memory_space=pl.ANY)
    return pl.pallas_call(
        functools.partial(kernel, ne, nd),
        out_shape=out_shape,
        in_specs=[anywhere] * len(args),
        out_specs=[anywhere] * len(out_shape),
        scratch_shapes=scratch,
        compiler_params=pltpu.CompilerParams(
            collective_id=collective_id, has_side_effects=True, vmem_limit_bytes=VMEM_BYTES
        ),
    )(*args)


def shards(ne, nd, tokens, cotangent, expert_ids, gate_prob, gate_weight, up_weight, down_weight):
    experts, depth, width = gate_weight.shape
    tok_rows, features = tokens.shape
    pair_count = tok_rows * TOPK
    capacity = max(2, 5 * pair_count // (4 * experts))
    slots = experts * capacity
    if depth % 256 == 0 and capacity % 8 == 0 and width % 16 == 0 and nd * slots % 256 == 0:
        weights = tuple(part.transpose(0, 2, 1) for part in (gate_weight, up_weight, down_weight))
        rows, grads, *landed = fused_dispatch(
            ne, nd, capacity,
            (tokens, cotangent, expert_ids.T, gate_prob) + weights,
            jax.ShapeDtypeStruct((nd, experts, capacity, features), jnp.bfloat16),
            jax.ShapeDtypeStruct((width, features), jnp.bfloat16),
        )
        total = nd * slots
        mixed_out, grad_tokens, *weight_grads = fused_combine(
            ne, nd, capacity,
            (rows.reshape(total, features), grads.reshape(total, features), *landed,
             expert_ids, gate_prob),
            jax.ShapeDtypeStruct(weights[0].shape, jnp.bfloat16),
        )
        return (mixed_out, grad_tokens, *(part.transpose(0, 2, 1) for part in weight_grads))
    slot_of = slot_index(expert_ids, experts, capacity)
    gate_scale = gate_prob.reshape(-1)
    send_rows = (
        jnp.zeros((slots, features), jnp.bfloat16).at[slot_of].set(jnp.repeat(tokens, TOPK, axis=0))
    )
    scaled = (gate_scale[:, None] * jnp.repeat(cotangent, TOPK, axis=0).astype(jnp.float32)).astype(
        jnp.bfloat16
    )
    send_grads = jnp.zeros((slots, features), jnp.bfloat16).at[slot_of].set(scaled)
    slot_shape = (experts, capacity, features)
    dma = pltpu.SemaphoreType.DMA
    pair_type = jax.ShapeDtypeStruct((nd,) + slot_shape, jnp.bfloat16)
    home_type = jax.ShapeDtypeStruct(slot_shape, jnp.bfloat16)
    weight_type = jax.ShapeDtypeStruct(gate_weight.shape, jnp.bfloat16)
    rows, grads, gate, up, down = comm_call(
        dispatch_kernel, ne, nd,
        (send_rows.reshape(slot_shape), send_grads.reshape(slot_shape),
         gate_weight, up_weight, down_weight),
        [pair_type] * 2 + [weight_type] * 3,
        [dma((2, ne)), dma((2, ne)), dma((3, ne)), dma((3, ne)),
         dma((2, nd, ne)), dma((2, nd, ne)), dma((5,))],
        0,
    )
    total = nd * slots
    rows, grads = rows.reshape(total, features), grads.reshape(total, features)
    gate, up, down = (part.reshape(features, width) for part in (gate, up, down))
    contracted = (((0,), (0,)), ((), ()))
    turned = (((1,), (1,)), ((), ()))

    def dot_by(left, right, dims):
        return lax.dot_general(left, right, dims, preferred_element_type=jnp.float32)

    ahead = (((1,), (0,)), ((), ()))
    pre_gate = dot_by(rows, gate, ahead)
    pre_up = dot_by(rows, up, ahead)
    hidden_grad = dot_by(grads, down, ahead)
    squash = jax.nn.sigmoid(pre_gate)
    hidden = (pre_gate * squash * pre_up).astype(jnp.bfloat16)
    gate_grad = (hidden_grad * pre_up * (squash * (1.0 + pre_gate * (1.0 - squash)))).astype(
        jnp.bfloat16
    )
    up_grad = (hidden_grad * (pre_gate * squash)).astype(jnp.bfloat16)
    totals = tuple(
        dot_by(left, right, contracted).astype(jnp.bfloat16).reshape(gate_weight.shape)
        for left, right in ((rows, gate_grad), (rows, up_grad), (grads, hidden))
    )
    outputs = dot_by(hidden, down, turned).astype(jnp.bfloat16)
    input_grads = (dot_by(gate_grad, gate, turned) + dot_by(up_grad, up, turned)).astype(jnp.bfloat16)
    out_home, in_home, grad_gate, grad_up, grad_down = comm_call(
        combine_kernel, ne, nd,
        (outputs.reshape((nd,) + slot_shape), input_grads.reshape((nd,) + slot_shape)) + totals,
        [home_type] * 2 + [weight_type] * 3,
        [pltpu.VMEM((2,) + slot_shape, jnp.bfloat16),
         pltpu.VMEM((2, nd - 1) + slot_shape, jnp.bfloat16),
         pltpu.VMEM((2,) + slot_shape, jnp.bfloat16),
         dma((2, ne)), dma((2, ne)), dma((3, ne)), dma((3, ne)),
         dma((2, nd, ne)), dma((2, nd, ne)), dma((2, ne)), dma((5,))],
        1,
    )
    out_pairs = out_home.reshape(slots, features)[slot_of].astype(jnp.float32)
    mixed_out = jnp.sum(
        (gate_scale[:, None] * out_pairs).reshape(tok_rows, TOPK, features), axis=1
    ).astype(jnp.bfloat16)
    in_pairs = in_home.reshape(slots, features)[slot_of].astype(jnp.float32)
    grad_tokens = jnp.sum(in_pairs.reshape(tok_rows, TOPK, features), axis=1).astype(jnp.bfloat16)
    return (mixed_out, grad_tokens, grad_gate, grad_up, grad_down)


def solution(mesh):
    by_token = P(("dp", "expert"), None)
    by_block = P(None, "expert", "dp")
    return jax.shard_map(
        functools.partial(shards, mesh.shape["expert"], mesh.shape["dp"]),
        mesh=mesh,
        in_specs=(by_token,) * 4 + (by_block,) * 3,
        out_specs=(by_token,) * 2 + (by_block,) * 3,
        check_vma=False,
    )
```
